128 devices in a mesh: dp: 2 (over y_hi), row: 16 (over x, z), col: 4 (over y_lo, core).
Axes of the slice: x: 4, y: 4 (y_hi: 2, y_lo: 2; y = y_hi * 2 + y_lo), z: 4, core: 2. Of those that a mesh axis runs over, the one named last changes fastest.
Arguments:
- params: float32 [2048, 36864], P('row', ('col', 'dp')), may hold values from -16 to 16
- grad_parts: bfloat16 [2, 2048, 36864], P('dp', 'row', 'col'), may hold values from -16 to 16
- row_moment: float32 [2048], P('row'), may hold values from 0.01 to 1
- col_moment: float32 [36864], P('col'), may hold values from 0.02 to 2
Outputs:
- new_params: float32 [2048, 36864], P('row', ('col', 'dp'))
- new_weights: bfloat16 [2048, 36864], P('row', 'col')
- new_row_moment: float32 [2048], P('row')
- new_col_moment: float32 [36864], P(('col', 'dp'))
- update: float32 [2048, 36864], P('row', ('col', 'dp'))
- clip_factor: float32 [], replicated
- param_scale: float32 [], replicated
The draws below stay inside these ranges and needn't reach their ends.
All inputs are finite; a program needn't handle non-finite values.
Results may differ from the reference program's by a relative error of at most 0.013.
Values may be sent and summed in bfloat16 or wider, within the bound.
No kernel may reach another device: no remote copies, remote signals or barrier semaphores. Data moves between devices by JAX's collectives and lax.ppermute only.
A program may use at most 64 MiB of HBM per device.

```python
import math
import jax
import jax.numpy as jnp
from jax import lax

R = 2048
C = 36864
STEP = 10
DP = 2
HALF_W = 4608


def scale_vector(key, count, lower, upper):
    spread = jnp.exp(jax.random.uniform(key, (count,), jnp.float32, math.log(lower), math.log(upper)))
    rising = jnp.exp(0.5 * math.log(3.0) * jnp.arange(count, dtype=jnp.float32) / count)
    return spread * rising


def column_boost(count, factor):
    position = jnp.arange(count, dtype=jnp.int32)
    upper_half = position // HALF_W % 2 == 1
    return jnp.where(upper_half, jnp.float32(factor), jnp.float32(1.0))


def draw_params(key, part):
    key = jax.random.fold_in(key, 11)
    first_key, second_key, third_key = jax.random.split(key, 3)
    normals = jax.random.normal(first_key, (R, C), jnp.float32)
    rows = scale_vector(second_key, R, 0.5, 2.0)
    boost = column_boost(C, 3.0)
    cols = scale_vector(third_key, C, 0.5, 2.0) * boost
    return jnp.clip(normals * rows[:, None] * cols[None, :], -16.0, 16.0)


def draw_grad_parts(key, part):
    key = jax.random.fold_in(key, 23)
    first_key, second_key, third_key = jax.random.split(key, 3)
    normals = jax.random.normal(first_key, (DP, R, C), jnp.float32)
    rows = scale_vector(second_key, R, 0.4, 2.5)
    boost = column_boost(C, 3.0)
    cols = scale_vector(third_key, C, 0.4, 2.5) * boost
    values = normals * rows[None, :, None] * cols[None, None, :]
    return jnp.clip(values, -16.0, 16.0).astype(jnp.bfloat16)


def levels(rng, dims, shards, low, largest):
    loudness = 1.0
    for axis_at, parts in shards:
        draws = jax.random.uniform(jax.random.fold_in(jax.random.fold_in(rng, 6), axis_at), (parts,), jnp.float32, low / len(shards), largest / len(shards))
        loudness = loudness * jnp.repeat(jnp.exp(draws), dims[axis_at] // parts).reshape((-1,) + (1,) * (len(dims) - 1 - axis_at))
    return loudness


def setup_inputs(seed: int = 0) -> dict:
    key_of = jax.random.split(jax.random.key(seed), 5)
    params = draw_params(jax.random.fold_in(key_of[4], 71), 0)
    grad_parts = draw_grad_parts(jax.random.fold_in(key_of[4], 71), 0)
    row_moment = jnp.clip(jnp.exp(math.log(1.0) - 4.6051702 * jax.random.uniform(key_of[2], (R,), jnp.float32) ** levels(key_of[2], (R,), ((0, 16),), -0.2, 0.2)), 0.01, 1.0)
    col_moment = jnp.clip(jnp.exp(math.log(2.0) - 4.6051702 * jax.random.uniform(key_of[3], (C,), jnp.float32) ** levels(key_of[3], (C,), ((0, 4),), -0.2, 0.2)), 0.02, 2.0)
    return dict(params=params, grad_parts=grad_parts, row_moment=row_moment, col_moment=col_moment)


def reference(params, grad_parts, row_moment, col_moment):
    decay_rate = 1.0 - STEP ** (-0.8)
    relative = min(0.01, STEP ** (-0.5))
    gradient = lax.optimization_barrier(jnp.sum(grad_parts.astype(jnp.float32), axis=0))
    squares = gradient * gradient + 1e-30
    new_rows = decay_rate * row_moment + (1.0 - decay_rate) * lax.optimization_barrier(jnp.mean(squares, axis=1))
    new_cols = decay_rate * col_moment + (1.0 - decay_rate) * lax.optimization_barrier(jnp.mean(squares, axis=0))
    row_mean = jnp.mean(new_rows)
    update = gradient * lax.rsqrt(new_rows[:, None] * new_cols[None, :] / row_mean)
    clip_factor = jnp.maximum(1.0, jnp.sqrt(jnp.mean(update * update)))
    param_scale = jnp.maximum(0.001, jnp.sqrt(jnp.mean(params * params)))
    step_size = relative * param_scale
    new_params = params - step_size / clip_factor * update
    return (new_params, new_params.astype(jnp.bfloat16), new_rows, new_cols, update, clip_factor, param_scale)
```

```python
import jax
import jax.numpy as jnp
from jax import lax
from jax.sharding import PartitionSpec as P

R = 2048
C = 36864
STEP = 10
CHUNKS = 4
SWAP = [(0, 1), (1, 0)]


def shards(params, grad_parts, row_moment, col_moment):
    decay_rate = 1.0 - STEP ** (-0.8)
    relative = min(0.01, STEP ** (-0.5))
    rows, width = params.shape
    step = width // CHUNKS
    position = lax.axis_index("dp")
    partial = grad_parts[0]

    def half(array, index, offset, size, axis):
        return lax.dynamic_slice_in_dim(array, index * width + offset, size, axis)

    pieces = []
    row_part = jnp.zeros((rows,), jnp.float32)
    col_parts = []
    received = [
        lax.ppermute(half(partial, 1 - position, k * step, step, 1), "dp", SWAP) for k in range(CHUNKS)
    ]
    for k in range(CHUNKS):
        piece = half(partial, position, k * step, step, 1).astype(jnp.float32) + received[k].astype(jnp.float32)
        squares = piece * piece + 1e-30
        row_part = row_part + jnp.sum(squares, axis=1)
        col_parts.append(jnp.sum(squares, axis=0))
        pieces.append(piece)
    gradient = jnp.concatenate(pieces, axis=1)
    col_part = jnp.concatenate(col_parts)
    weight_part = jnp.sum(params * params)

    sent = jnp.broadcast_to(row_part[None, None, :], (8, 1, rows))
    row_totals = jnp.sum(lax.all_to_all(sent, ("dp", "col"), 0, 0), axis=(0, 1))
    new_rows = decay_rate * row_moment + (1.0 - decay_rate) * (row_totals / C)

    sent = jnp.broadcast_to(col_part.astype(jnp.bfloat16).reshape(1, width // 128, 128), (16, width // 128, 128))
    got = lax.all_to_all(sent, "row", 0, 0)
    col_totals = jnp.sum(got.astype(jnp.float32), axis=0).reshape(width)
    old_cols = half(col_moment, position, 0, width, 0)
    new_cols = decay_rate * old_cols + (1.0 - decay_rate) * (col_totals / R)

    scaled = gradient * gradient * (1.0 / new_rows)[:, None] * (1.0 / new_cols)[None, :]
    sums = jnp.stack([jnp.sum(scaled), weight_part, jnp.sum(new_rows)])
    sums = jnp.pad(sums, (0, 125))
    sent = jnp.broadcast_to(sums[None, None, :], (128, 1, 128))
    totals = jnp.sum(lax.all_to_all(sent, ("dp", "row", "col"), 0, 0), axis=(0, 1))
    row_mean = totals[2] / (8 * R)
    clip_factor = jnp.maximum(1.0, jnp.sqrt(totals[0] * row_mean / (R * C)))
    param_scale = jnp.maximum(0.001, jnp.sqrt(totals[1] / (R * C)))
    step_size = relative * param_scale / clip_factor

    update = gradient * lax.rsqrt(new_rows / row_mean)[:, None] * lax.rsqrt(new_cols)[None, :]
    new_params = params - step_size * update
    own = new_params.astype(jnp.bfloat16)
    new_weights = jnp.zeros((rows, 2 * width), jnp.bfloat16)
    others = [lax.ppermute(own[:, k * step : (k + 1) * step], "dp", SWAP) for k in range(CHUNKS)]
    new_weights = lax.dynamic_update_slice_in_dim(new_weights, own, position * width, 1)
    for k in range(CHUNKS):
        new_weights = lax.dynamic_update_slice_in_dim(
            new_weights, others[k], (1 - position) * width + k * step, 1
        )
    return (new_params, new_weights, new_rows, new_cols, update, clip_factor, param_scale)


def solution(mesh):
    in_specs = (P("row", ("col", "dp")), P("dp", "row", "col"), P("row"), P("col"))
    out_specs = (
        P("row", ("col", "dp")),
        P("row", "col"),
        P("row"),
        P(("col", "dp")),
        P("row", ("col", "dp")),
        P(),
        P(),
    )
    return jax.shard_map(shards, mesh=mesh, in_specs=in_specs, out_specs=out_specs, check_vma=False)
```

```python
import functools

import jax
import jax.numpy as jnp
from jax import lax
from jax.experimental import pallas as pl
from jax.experimental.pallas import tpu as pltpu
from jax.sharding import PartitionSpec as P

R = 2048
C = 36864
STEP = 10
DECAY = 1.0 - STEP ** (-0.8)
RELATIVE = min(0.01, STEP ** (-0.5))
LANES = 128
SWAP = [(0, 1), (1, 0)]
PIECES = 4
BLOCK = 512
EARLY = 3
LATE = (4, 2)
VMEM_LIMIT = 24 << 20
f32, bf16 = jnp.float32, jnp.bfloat16
shape = jax.ShapeDtypeStruct


def down(row):
    return jnp.broadcast_to(row, (LANES, LANES)).T


def flat(acc):
    return jnp.sum(acc.T, axis=0, keepdims=True)


def tile(at):
    return slice(at * LANES, (at + 1) * LANES)


def sums_kernel(mine_ref, got_ref, grad_ref, row_ref, sent_ref, acc_ref, cols_ref):
    k = pl.program_id(0)
    tiles = got_ref.shape[1] // LANES

    @pl.when(k == 0)
    def _():
        acc_ref[...] = jnp.zeros_like(acc_ref)
        cols_ref[...] = jnp.zeros_like(cols_ref)

    acc = acc_ref[...]
    for t in range(tiles):
        g = mine_ref[:, tile(t)].astype(f32) + got_ref[:, tile(t)].astype(f32)
        grad_ref[:, tile(t)] = g
        squares = g * g + 1e-30
        acc = acc + squares
        cols_ref[pl.ds(k * tiles + t, 1), :] = jnp.sum(squares, axis=0, keepdims=True)
    acc_ref[...] = acc

    @pl.when(k == pl.num_programs(0) - 1)
    def _():
        row_ref[...] = flat(acc_ref[...])
        sent = cols_ref[...].astype(bf16)
        for peer in range(sent_ref.shape[0]):
            sent_ref[peer] = sent


def moments_kernel(
    grad_ref, got_ref, row_ref, old_rows_ref, old_cols_ref, weight_ref,
    new_cols_ref, copy_ref, sent_ref, inv_cols, acc_ref,
):
    k = pl.program_id(0)
    height = new_cols_ref.shape[0]
    tiles = grad_ref.shape[1] // LANES

    @pl.when(k == 0)
    def _():
        totals = got_ref[0].astype(f32)
        for peer in range(1, got_ref.shape[0]):
            totals = totals + got_ref[peer].astype(f32)
        new_cols = DECAY * old_cols_ref[...] + (1.0 - DECAY) * (totals[:height] / R)
        new_cols_ref[...] = new_cols
        copy_ref[...] = new_cols
        inv_cols[...] = 1.0 / new_cols
        acc_ref[...] = jnp.zeros_like(acc_ref)

    acc = acc_ref[...]
    for t in range(tiles):
        g = grad_ref[:, tile(t)]
        acc = acc + g * g * inv_cols[pl.ds(k * tiles + t, 1), :]
    acc_ref[...] = acc

    @pl.when(k == pl.num_programs(0) - 1)
    def _():
        at = lax.broadcasted_iota(jnp.int32, (4, LANES), 0)
        rows = [row_ref[...], flat(acc_ref[...]), old_rows_ref[...], jnp.full((1, LANES), weight_ref[0, 0])]
        sent = jnp.zeros((4, LANES), f32)
        for i, row in enumerate(rows):
            sent = jnp.where(at == i, jnp.broadcast_to(row, (4, LANES)), sent)
        sent_ref[...] = jnp.broadcast_to(sent[None], sent_ref.shape)


def weights_block(grad_ref, params_ref, out_ref, row_scale, col_scale, step_size, first, to=0):
    for t in range(grad_ref.shape[1] // LANES):
        update = grad_ref[:, tile(t)] * row_scale * col_scale[pl.ds(first + t, 1), :]
        new = (params_ref[:, tile(t)] - step_size * update).astype(bf16)
        out_ref[:, pl.ds(pl.multiple_of(to + t * LANES, LANES), LANES)] = new


def first_weights_kernel(
    at_ref, got_ref, cols_ref, grad_ref, params_ref,
    out_ref, rows_ref, clip_ref, scale_ref, step_ref, row_scale, col_scale, all_rows,
):
    k = pl.program_id(0)

    @pl.when(k == 0)
    def _():
        update_sum = jnp.zeros((1, LANES), f32)
        row_sum = jnp.zeros((1, LANES), f32)
        weight_sum = jnp.zeros((1, LANES), f32)
        for block in range(16):
            got = None
            for d in range(2):
                for c in range(4):
                    term = got_ref[d * 64 + block * 4 + c]
                    got = term if got is None else got + term
            rows = DECAY * got_ref[block * 4][2:3] + (1.0 - DECAY) * (got[0:1] / C)
            all_rows[block : block + 1, :] = rows
            update_sum = update_sum + got[1:2] / rows
            row_sum = row_sum + rows
            weight_sum = weight_sum + got[3:4]
        row_mean = jnp.sum(row_sum, axis=1, keepdims=True) / R
        rows = all_rows[pl.ds(at_ref[1], 1), :]
        rows_ref[...] = rows
        row_scale[...] = down(lax.rsqrt(rows / row_mean))
        col_scale[...] = lax.rsqrt(cols_ref[...])
        update_mean = jnp.sum(update_sum, axis=1, keepdims=True) * row_mean / (R * C)
        weight_mean = weight_sum[:, :1] / (R * C)
        clip_factor = jnp.maximum(1.0, jnp.sqrt(update_mean))
        param_scale = jnp.maximum(0.001, jnp.sqrt(weight_mean))
        clip_ref[...] = clip_factor
        scale_ref[...] = param_scale
        step_ref[...] = RELATIVE * param_scale / clip_factor
        if EARLY:
            scale = jnp.zeros((LANES, LANES), f32)
            for t in range(EARLY * BLOCK // LANES):
                scale_cols = jnp.broadcast_to(col_scale[t : t + 1, :], (LANES, LANES))
                scale = jnp.where(lax.broadcasted_iota(jnp.int32, scale.shape, 0) == t, scale_cols, scale)
            out_ref[:, pl.ds(LATE[0] * BLOCK, LANES)] = scale.astype(bf16)

    first = (EARLY + k) * (BLOCK // LANES)
    weights_block(grad_ref, params_ref, out_ref, row_scale[...], col_scale, step_ref[...], first, k * BLOCK)


def weights_kernel(start, grad_ref, params_ref, row_scale, col_scale, step_ref, out_ref):
    first = (start + pl.program_id(0)) * (BLOCK // LANES)
    weights_block(grad_ref, params_ref, out_ref, row_scale[...], col_scale, step_ref[...], first)


def params_kernel(at_ref, grad_ref, params_ref, row_scale, col_scale, step_ref, new_ref, update_ref, weights_ref):
    first = pl.program_id(0) * (BLOCK // LANES)
    across, step_size = row_scale[...], step_ref[...]
    for t in range(BLOCK // LANES):
        update = grad_ref[:, tile(t)] * across * col_scale[pl.ds(first + t, 1), :]
        new = params_ref[:, tile(t)] - step_size * update
        update_ref[:, tile(t)] = update
        new_ref[:, tile(t)] = new
        weights_ref[:, tile(t)] = new.astype(bf16)


def early_kernel(at_ref, mine_ref, grad_ref, params_ref, row_scale, cols_ref, step_ref, _, out_ref, scale_ref):
    k = pl.program_id(0)

    @pl.when(k == 0)
    def _():
        scale_ref[...] = cols_ref[...].astype(f32)

    first = k * (BLOCK // LANES)
    across, step_size = row_scale[...], step_ref[...]
    for t in range(BLOCK // LANES):
        g = mine_ref[0, :, tile(t)].astype(f32) + grad_ref[:, tile(t)].astype(f32)
        update = g * across * scale_ref[pl.ds(first + t, 1), :]
        out_ref[:, tile(t)] = (params_ref[:, tile(t)].astype(f32) - step_size * update).astype(bf16)


def place_kernel(at_ref, got_ref, _, out_ref):
    out_ref[...] = got_ref[...]


def whole(*dims):
    return pl.BlockSpec(dims, lambda *_: (0,) * len(dims))


def call(kernel, grid, ins, outs, args, nbytes, scratch=(), at=None, aliases=None):
    prefetch = () if at is None else (at,)
    return pl.pallas_call(
        kernel,
        grid_spec=pltpu.PrefetchScalarGridSpec(
            num_scalar_prefetch=len(prefetch), grid=(grid,), in_specs=ins,
            out_specs=[spec for spec, _ in outs], scratch_shapes=list(scratch),
        ),
        out_shape=[out for _, out in outs],
        input_output_aliases=aliases or {},
        cost_estimate=pl.CostEstimate(flops=nbytes, bytes_accessed=nbytes, transcendentals=0),
        compiler_params=pltpu.CompilerParams(vmem_limit_bytes=VMEM_LIMIT),
    )(*prefetch, *args)


def shards(params, grad_parts, row_moment, col_moment):
    rows, width = params.shape
    height = width // LANES
    padded = -(-height // 16) * 16
    piece = width // PIECES
    blocks = width // BLOCK
    position = lax.axis_index("dp")
    other = 1 - position
    at = jnp.stack([position, lax.axis_index("row")]).astype(jnp.int32)
    any_spec = pl.BlockSpec(memory_space=pl.ANY)
    row_spec, col_spec, one_spec = whole(1, rows), whole(height, LANES), whole(1, 1)
    square = whole(rows, LANES)
    block_at = lambda first: pl.BlockSpec((rows, BLOCK), lambda k, *_: (0, first + k))

    outgoing = lax.dynamic_slice_in_dim(grad_parts[0], other * width, width, 1)
    got = lax.ppermute(outgoing, "dp", SWAP)
    later, later_params, later_cols, _ = lax.optimization_barrier((grad_parts[0], params, col_moment, outgoing))
    mine = lax.dynamic_slice_in_dim(later, position * width, width, 1)
    parts = lax.dynamic_slice_in_dim(later, position * width, EARLY * BLOCK, 1)
    ahead = jnp.concatenate([parts, later_params[:, : EARLY * BLOCK].astype(bf16)], axis=1)
    ahead = lax.ppermute(ahead, "dp", SWAP)
    weight_part = jnp.sum(later_params * later_params).reshape(1, 1)
    old_cols = lax.dynamic_slice_in_dim(later_cols, position * width, width, 0).reshape(height, LANES)
    got, mine, weight_part, old_cols, at = lax.optimization_barrier((got, mine, weight_part, old_cols, at))

    part = pl.BlockSpec((rows, piece), lambda k: (0, k))
    gradient, row_part, sent = call(
        sums_kernel, PIECES, [part, part],
        [(part, shape((rows, width), f32)), (row_spec, shape((1, rows), f32)),
         (whole(16, padded, LANES), shape((16, padded, LANES), bf16))],
        (mine, got), 8 * rows * width,
        [pltpu.VMEM((rows, LANES), f32), pltpu.VMEM((padded, LANES), f32)],
    )

    col_parts = lax.all_to_all(sent, "row", 0, 0)
    wide = pl.BlockSpec((rows, 3 * BLOCK), lambda k: (0, k))
    new_cols, cols_copy, sent = call(
        moments_kernel, blocks // 3,
        [wide, whole(16, padded, LANES), row_spec, row_spec, col_spec, pl.BlockSpec(memory_space=pltpu.SMEM)],
        [(col_spec, shape((height, LANES), f32))] * 2 + [(whole(128, 4, LANES), shape((128, 4, LANES), f32))],
        (gradient, col_parts, row_part, row_moment.reshape(1, rows), old_cols, weight_part), 4 * rows * width,
        [pltpu.VMEM((height, LANES), f32), pltpu.VMEM((rows, LANES), f32)],
    )
    sent, ahead = lax.optimization_barrier((sent, ahead))
    parts = lax.all_to_all(sent, ("dp", "row", "col"), 0, 0)
    sent_width = LATE[0] * BLOCK + (LANES if EARLY else 0)
    out, new_rows, clip_factor, param_scale, step_size, row_scale, col_scale = call(
        first_weights_kernel, LATE[0],
        [whole(128, 4, LANES), col_spec, block_at(EARLY), block_at(EARLY)],
        [(whole(rows, sent_width), shape((rows, sent_width), bf16)), (row_spec, shape((1, rows), f32)),
         (one_spec, shape((1, 1), f32)), (one_spec, shape((1, 1), f32)), (one_spec, shape((1, 1), f32)),
         (square, shape((rows, LANES), f32)), (col_spec, shape((height, LANES), f32))],
        (parts, cols_copy, gradient, params), 4 * rows * LATE[0] * BLOCK,
        [pltpu.VMEM((16, LANES), f32)], at,
    )
    late = [lax.ppermute(out, "dp", SWAP)]
    start = EARLY + LATE[0]
    for count in LATE[1:]:
        (out,) = call(
            functools.partial(weights_kernel, start), count,
            [block_at(start), block_at(start), square, col_spec, one_spec],
            [(block_at(0), shape((rows, count * BLOCK), bf16))],
            (gradient, params, row_scale, col_scale, step_size), 4 * rows * count * BLOCK,
        )
        late.append(lax.ppermute(out, "dp", SWAP))
        start += count

    new_params, update, new_weights = call(
        params_kernel, blocks,
        [block_at(0), block_at(0), square, col_spec, one_spec],
        [(block_at(0), shape((rows, width), f32)), (block_at(0), shape((rows, width), f32)),
         (pl.BlockSpec((rows, BLOCK), lambda k, at: (0, at[0] * blocks + k)), shape((rows, 2 * width), bf16))],
        (gradient, params, row_scale, col_scale, step_size), 18 * rows * width, (), at,
    )
    out_shape = shape((rows, 2 * width), bf16)
    (new_weights,) = call(
        early_kernel, EARLY,
        [pl.BlockSpec((1, rows, BLOCK), lambda k, at: (0, 0, (1 - at[0]) * blocks + k)),
         block_at(0), block_at(EARLY), square,
         pl.BlockSpec((rows, LANES), lambda *_: (0, LATE[0] * BLOCK // LANES)), one_spec, any_spec],
        [(pl.BlockSpec((rows, BLOCK), lambda k, at: (0, (1 - at[0]) * blocks + k)), out_shape)],
        (grad_parts, ahead, ahead, row_scale, late[0], step_size, new_weights),
        8 * rows * EARLY * BLOCK, [pltpu.VMEM((rows, LANES), f32)], at, {7: 0},
    )
    start = EARLY
    for count, values in zip(LATE, late):
        (new_weights,) = call(
            place_kernel, count, [block_at(0), any_spec],
            [(pl.BlockSpec((rows, BLOCK), lambda k, at, s=start: (0, (1 - at[0]) * blocks + s + k)), out_shape)],
            (values, new_weights), 4 * rows * count * BLOCK, (), at, {2: 0},
        )
        start += count
    return (
        new_params, new_weights, new_rows.reshape(rows), new_cols.reshape(width), update,
        clip_factor.reshape(()), param_scale.reshape(()),
    )


def solution(mesh):
    in_specs = (P("row", ("col", "dp")), P("dp", "row", "col"), P("row"), P("col"))
    out_specs = (
        P("row", ("col", "dp")),
        P("row", "col"),
        P("row"),
        P(("col", "dp")),
        P("row", ("col", "dp")),
        P(),
        P(),
    )
    return jax.shard_map(shards, mesh=mesh, in_specs=in_specs, out_specs=out_specs, check_vma=False)
```

```python
import functools

import jax
import jax.numpy as jnp
from jax import lax
from jax.experimental import pallas as pl
from jax.experimental.pallas import tpu as pltpu
from jax.sharding import PartitionSpec as P

R = 2048
C = 36864
STEP = 10
DECAY = 1.0 - STEP ** (-0.8)
RELATIVE = min(0.01, STEP ** (-0.5))
LANES = 128
SWAP = [(0, 1), (1, 0)]
BLOCK = 512
WIDE = 1536
AHEAD = (3, 2)
EARLY = sum(AHEAD)
LATE = (2, 2)
VMEM_LIMIT = 24 << 20
f32, bf16 = jnp.float32, jnp.bfloat16
shape = jax.ShapeDtypeStruct


def down(row):
    return jnp.broadcast_to(row, (LANES, LANES)).T


def flat(acc):
    return jnp.sum(acc.T, axis=0, keepdims=True)


def tile(at):
    return slice(at * LANES, (at + 1) * LANES)


def span(start, count):
    return pl.ds(pl.multiple_of(start, LANES), count)


def begin(*copies):
    copies = [pltpu.make_async_copy(*copy) for copy in copies]
    for copy in copies:
        copy.start()
    return copies


def steps(width):
    return [(start, WIDE) for start in range(0, width, WIDE)]


def half_kernel(grad_ref, out_ref, buf, in_sems, out_sems):
    width = buf.shape[1]
    other = (1 - lax.axis_index("dp")) * width
    pieces = steps(width)
    ins = [
        begin((grad_ref.at[0, :, span(other + s, n)], buf.at[:, s : s + n], in_sems.at[i]))[0]
        for i, (s, n) in enumerate(pieces)
    ]
    outs = []
    for i, (s, n) in enumerate(pieces):
        ins[i].wait()
        outs += begin((buf.at[:, s : s + n], out_ref.at[:, s : s + n], out_sems.at[i]))
    for copy in outs:
        copy.wait()


def prepare_kernel(grad_ref, params_ref, _, *refs):
    ahead_refs, (weight_ref, params, parts, values, sems, out_sems) = refs[: len(AHEAD)], refs[len(AHEAD) :]
    width = params.shape[1]
    mine = lax.axis_index("dp") * width
    pieces = steps(width)
    ins = [
        begin((params_ref.at[:, s : s + n], params.at[:, s : s + n], sems.at[i]))[0] for i, (s, n) in enumerate(pieces)
    ]
    grad = begin((grad_ref.at[0, :, span(mine, EARLY * BLOCK)], parts, sems.at[len(pieces)]))[0]
    acc = jnp.zeros((LANES, LANES), f32)
    for i, (s, n) in enumerate(pieces):
        ins[i].wait()
        for t in range(s // LANES, (s + n) // LANES):
            value = params[:, tile(t)]
            acc = acc + value * value
            if t < EARLY * BLOCK // LANES:
                values[:, tile(t)] = value.astype(bf16)
    grad.wait()
    outs, start = [], 0
    for i, (count, ahead_ref) in enumerate(zip(AHEAD, ahead_refs)):
        n = count * BLOCK
        outs += begin(
            (parts.at[:, start : start + n], ahead_ref.at[:, 0:n], out_sems.at[2 * i]),
            (values.at[:, start : start + n], ahead_ref.at[:, n : 2 * n], out_sems.at[2 * i + 1]),
        )
        start += n
    weight_ref[...] = jnp.sum(jnp.sum(acc, axis=0, keepdims=True), axis=1, keepdims=True)
    for copy in outs:
        copy.wait()


def sums_kernel(grad_parts_ref, got_ref, _, grad_ref, row_ref, sent_ref, mine, got, grad, cols, sems, out_sems):
    width = grad.shape[1]
    first = lax.axis_index("dp") * width
    pieces = steps(width)
    ins = [
        begin(
            (grad_parts_ref.at[0, :, span(first + s, n)], mine.at[:, s : s + n], sems.at[2 * i]),
            (got_ref.at[:, s : s + n], got.at[:, s : s + n], sems.at[2 * i + 1]),
        )
        for i, (s, n) in enumerate(pieces)
    ]
    cols[...] = jnp.zeros_like(cols)
    acc = jnp.zeros((LANES, LANES), f32)
    outs = []
    for i, (s, n) in enumerate(pieces):
        for copy in ins[i]:
            copy.wait()
        for t in range(s // LANES, (s + n) // LANES):
            g = mine[:, tile(t)].astype(f32) + got[:, tile(t)].astype(f32)
            grad[:, tile(t)] = g
            squares = g * g + 1e-30
            acc = acc + squares
            cols[t : t + 1, :] = jnp.sum(squares, axis=0, keepdims=True)
        outs += begin((grad.at[:, s : s + n], grad_ref.at[:, s : s + n], out_sems.at[i]))
    row_ref[...] = flat(acc)
    sent = cols[...].astype(bf16)
    for peer in range(sent_ref.shape[0]):
        sent_ref[peer] = sent
    for copy in outs:
        copy.wait()


def moments_kernel(
    grad_ref, got_ref, row_ref, old_rows_ref, old_cols_ref, weight_ref,
    new_cols_ref, copy_ref, sent_ref, grad, inv_cols, sent, sems, out_sem,
):
    width = grad.shape[1]
    height = width // LANES
    pieces = steps(width)
    ins = [begin((grad_ref.at[:, s : s + n], grad.at[:, s : s + n], sems.at[i]))[0] for i, (s, n) in enumerate(pieces)]
    totals = got_ref[0].astype(f32)
    for peer in range(1, got_ref.shape[0]):
        totals = totals + got_ref[peer].astype(f32)
    old_cols = jnp.where(lax.axis_index("dp") == 0, old_cols_ref[:height], old_cols_ref[height:])
    new_cols = DECAY * old_cols + (1.0 - DECAY) * (totals[:height] / R)
    new_cols_ref[...] = new_cols
    copy_ref[...] = new_cols
    inv_cols[...] = 1.0 / new_cols
    acc = jnp.zeros((LANES, LANES), f32)
    for i, (s, n) in enumerate(pieces):
        ins[i].wait()
        for t in range(s // LANES, (s + n) // LANES):
            g = grad[:, tile(t)]
            acc = acc + g * g * inv_cols[t : t + 1, :]
    at = lax.broadcasted_iota(jnp.int32, (4, LANES), 0)
    value = jnp.zeros((4, LANES), f32)
    for i, row in enumerate([row_ref[...], flat(acc), old_rows_ref[...], weight_ref[...]]):
        value = jnp.where(at == i, jnp.broadcast_to(row, (4, LANES)), value)
    sent[...] = jnp.broadcast_to(value[None], sent.shape)
    (copy,) = begin((sent, sent_ref, out_sem))
    copy.wait()


def weights_piece(grad, params, out_ref, row_scale, col_scale, step_size, first):
    for t in range(grad.shape[1] // LANES):
        update = grad[:, tile(t)] * row_scale * col_scale[first + t : first + t + 1, :]
        out_ref[:, tile(t)] = (params[:, tile(t)] - step_size * update).astype(bf16)


def first_weights_kernel(
    got_ref, cols_ref, grad_ref, params_ref,
    out_ref, rows_ref, clip_ref, scale_ref, step_ref, row_scale, col_scale, grad, params, all_rows, sems,
):
    start, count = EARLY * BLOCK, grad.shape[1]
    ins = begin(
        (grad_ref.at[:, start : start + count], grad, sems.at[0]),
        (params_ref.at[:, start : start + count], params, sems.at[1]),
    )
    update_sum = jnp.zeros((1, LANES), f32)
    row_sum = jnp.zeros((1, LANES), f32)
    weight_sum = jnp.zeros((1, LANES), f32)
    for block in range(16):
        got = None
        for d in range(2):
            for c in range(4):
                term = got_ref[d * 64 + block * 4 + c]
                got = term if got is None else got + term
        rows = DECAY * got_ref[block * 4][2:3] + (1.0 - DECAY) * (got[0:1] / C)
        all_rows[block : block + 1, :] = rows
        update_sum = update_sum + got[1:2] / rows
        row_sum = row_sum + rows
        weight_sum = weight_sum + got[3:4]
    row_mean = jnp.sum(row_sum, axis=1, keepdims=True) / R
    rows = all_rows[pl.ds(lax.axis_index("row"), 1), :]
    rows_ref[...] = rows
    row_scale[...] = down(lax.rsqrt(rows / row_mean))
    col_scale[...] = lax.rsqrt(cols_ref[...])
    update_mean = jnp.sum(update_sum, axis=1, keepdims=True) * row_mean / (R * C)
    weight_mean = weight_sum[:, :1] / (R * C)
    clip_factor = jnp.maximum(1.0, jnp.sqrt(update_mean))
    param_scale = jnp.maximum(0.001, jnp.sqrt(weight_mean))
    clip_ref[...] = clip_factor
    scale_ref[...] = param_scale
    step_size = RELATIVE * param_scale / clip_factor
    step_ref[...] = step_size
    scale = jnp.zeros((LANES, LANES), f32)
    at = lax.broadcasted_iota(jnp.int32, scale.shape, 0)
    for t in range(EARLY * BLOCK // LANES):
        scale = jnp.where(at == t, jnp.broadcast_to(col_scale[t : t + 1, :], scale.shape), scale)
    out_ref[:, count : count + LANES] = scale.astype(bf16)
    for copy in ins:
        copy.wait()
    weights_piece(grad, params, out_ref, row_scale[...], col_scale, step_size, start // LANES)


def weights_kernel(start, grad_ref, params_ref, row_scale, col_scale, step_ref, out_ref, grad, params, sems):
    count = grad.shape[1]
    ins = begin(
        (grad_ref.at[:, start : start + count], grad, sems.at[0]),
        (params_ref.at[:, start : start + count], params, sems.at[1]),
    )
    for copy in ins:
        copy.wait()
    weights_piece(grad, params, out_ref, row_scale[...], col_scale, step_ref[...], start // LANES)


def params_kernel(
    grad_ref, params_ref, row_scale, col_scale, step_ref,
    new_ref, update_ref, weights_ref, grad, params, update, new, weights, sems, out_sems,
):
    width = grad.shape[1]
    mine = lax.axis_index("dp") * width
    pieces = steps(width)
    ins = [
        begin(
            (grad_ref.at[:, s : s + n], grad.at[:, s : s + n], sems.at[2 * i]),
            (params_ref.at[:, s : s + n], params.at[:, s : s + n], sems.at[2 * i + 1]),
        )
        for i, (s, n) in enumerate(pieces)
    ]
    across, step_size = row_scale[...], step_ref[...]
    outs = []
    for i, (s, n) in enumerate(pieces):
        for copy in ins[i]:
            copy.wait()
        for t in range(s // LANES, (s + n) // LANES):
            value = grad[:, tile(t)] * across * col_scale[t : t + 1, :]
            moved = params[:, tile(t)] - step_size * value
            update[:, tile(t)] = value
            new[:, tile(t)] = moved
            weights[:, tile(t)] = moved.astype(bf16)
        outs += begin(
            (update.at[:, s : s + n], update_ref.at[:, s : s + n], out_sems.at[3 * i]),
            (new.at[:, s : s + n], new_ref.at[:, s : s + n], out_sems.at[3 * i + 1]),
            (weights.at[:, s : s + n], weights_ref.at[:, span(mine + s, n)], out_sems.at[3 * i + 2]),
        )
    for copy in outs:
        copy.wait()


def early_kernel(start, width, grad_ref, ahead_ref, row_scale, late_ref, step_ref, _, out_ref,
                 mine, got, scale, out, scales, sems, out_sem):
    count = mine.shape[1]
    first = (1 - lax.axis_index("dp")) * width + start
    ins = begin(
        (late_ref.at[:, LATE[0] * BLOCK : LATE[0] * BLOCK + LANES], scale, sems.at[0]),
        (grad_ref.at[0, :, span(first, count)], mine, sems.at[1]),
        (ahead_ref, got, sems.at[2]),
    )
    across, step_size = row_scale[...], step_ref[...]
    for copy in ins:
        copy.wait()
    scales[...] = scale[...].astype(f32)
    for t in range(count // LANES):
        g = mine[:, tile(t)].astype(f32) + got[:, tile(t)].astype(f32)
        at = start // LANES + t
        update = g * across * scales[at : at + 1, :]
        out[:, tile(t)] = (got[:, tile(count // LANES + t)].astype(f32) - step_size * update).astype(bf16)
    (copy,) = begin((out, out_ref.at[:, span(first, count)], out_sem))
    copy.wait()


def place_kernel(start, width, got_ref, _, out_ref, got, sems):
    first = (1 - lax.axis_index("dp")) * width + start
    count = got.shape[1]
    (copy,) = begin((got_ref.at[:, 0:count], got, sems.at[0]))
    copy.wait()
    (copy,) = begin((got, out_ref.at[:, span(first, count)], sems.at[1]))
    copy.wait()


HBM, VMEM = pltpu.HBM, pltpu.VMEM
dma = pltpu.SemaphoreType.DMA


def call(kernel, ins, outs, scratch, args, nbytes, aliases=None):
    return pl.pallas_call(
        kernel,
        in_specs=[pl.BlockSpec(memory_space=space) for space in ins],
        out_specs=[pl.BlockSpec(memory_space=space) for space, _ in outs],
        out_shape=[out for _, out in outs],
        scratch_shapes=list(scratch),
        input_output_aliases=aliases or {},
        cost_estimate=pl.CostEstimate(flops=nbytes, bytes_accessed=nbytes, transcendentals=0),
        compiler_params=pltpu.CompilerParams(vmem_limit_bytes=VMEM_LIMIT),
    )(*args)


def shards(params, grad_parts, row_moment, col_moment):
    rows, width = params.shape
    height = width // LANES
    padded = -(-height // 16) * 16
    early = EARLY * BLOCK
    count = len(steps(width))

    (outgoing,) = call(
        half_kernel, [HBM], [(HBM, shape((rows, width), bf16))],
        [VMEM((rows, width), bf16), dma((count,)), dma((count,))], (grad_parts,), 4 * rows * width,
    )
    got = lax.ppermute(outgoing, "dp", SWAP)
    *ahead, weight_part = call(
        prepare_kernel, [HBM, HBM, HBM],
        [(HBM, shape((rows, 2 * n * BLOCK), bf16)) for n in AHEAD] + [(VMEM, shape((1, 1), f32))],
        [VMEM((rows, width), f32), VMEM((rows, early), bf16), VMEM((rows, early), bf16), dma((count + 1,)),
         dma((2 * len(AHEAD),))],
        (grad_parts, params, outgoing), 4 * rows * (width + early),
    )
    arrived = [lax.ppermute(ahead[0], "dp", SWAP)]

    gradient, row_part, sent = call(
        sums_kernel, [HBM, HBM, VMEM],
        [(HBM, shape((rows, width), f32)), (VMEM, shape((1, rows), f32)),
         (VMEM, shape((16, padded, LANES), bf16))],
        [VMEM((rows, width), bf16), VMEM((rows, width), bf16), VMEM((rows, width), f32), VMEM((padded, LANES), f32),
         dma((2 * count,)), dma((count,))],
        (grad_parts, got, weight_part), 8 * rows * width,
    )
    col_parts = lax.all_to_all(sent, "row", 0, 0)
    new_cols, cols_copy, sent = call(
        moments_kernel, [HBM] + [VMEM] * 5,
        [(VMEM, shape((height, LANES), f32)), (VMEM, shape((height, LANES), f32)),
         (HBM, shape((128, 4, LANES), f32))],
        [VMEM((rows, width), f32), VMEM((height, LANES), f32), VMEM((128, 4, LANES), f32), dma((count,)), dma],
        (gradient, col_parts, row_part, row_moment.reshape(1, rows), col_moment.reshape(2 * height, LANES), weight_part),
        4 * rows * width,
    )
    sent, arrived[0], *ahead = lax.optimization_barrier((sent, arrived[0], *ahead))
    parts = lax.all_to_all(sent, ("dp", "row", "col"), 0, 0)
    arrived += [lax.ppermute(values, "dp", SWAP) for values in ahead[1:]]

    n = LATE[0] * BLOCK
    out, new_rows, clip_factor, param_scale, step_size, row_scale, col_scale = call(
        first_weights_kernel, [VMEM, VMEM, HBM, HBM],
        [(VMEM, shape((rows, n + LANES), bf16)), (VMEM, shape((1, rows), f32)),
         (VMEM, shape((1, 1), f32)), (VMEM, shape((1, 1), f32)), (VMEM, shape((1, 1), f32)),
         (VMEM, shape((rows, LANES), f32)), (VMEM, shape((height, LANES), f32))],
        [VMEM((rows, n), f32), VMEM((rows, n), f32), VMEM((16, LANES), f32), dma((2,))],
        (parts, cols_copy, gradient, params), 8 * rows * n,
    )
    late = [lax.ppermute(out, "dp", SWAP)]
    start = early + n
    for blocks in LATE[1:]:
        n = blocks * BLOCK
        (out,) = call(
            functools.partial(weights_kernel, start), [HBM, HBM, VMEM, VMEM, VMEM],
            [(VMEM, shape((rows, n), bf16))], [VMEM((rows, n), f32), VMEM((rows, n), f32), dma((2,))],
            (gradient, params, row_scale, col_scale, step_size), 8 * rows * n,
        )
        late.append(lax.ppermute(out, "dp", SWAP))
        start += n

    out_shape = shape((rows, 2 * width), bf16)
    new_params, update, new_weights = call(
        params_kernel, [HBM, HBM, VMEM, VMEM, VMEM],
        [(HBM, shape((rows, width), f32)), (HBM, shape((rows, width), f32)), (HBM, out_shape)],
        [VMEM((rows, width), f32)] * 4 + [VMEM((rows, width), bf16), dma((2 * count,)), dma((3 * count,))],
        (gradient, params, row_scale, col_scale, step_size), 18 * rows * width,
    )
    start = 0
    for blocks, values in zip(AHEAD, arrived):
        n = blocks * BLOCK
        (new_weights,) = call(
            functools.partial(early_kernel, start, width), [HBM, HBM, VMEM, HBM, VMEM, HBM], [(HBM, out_shape)],
            [VMEM((rows, n), bf16), VMEM((rows, 2 * n), bf16), VMEM((rows, LANES), bf16), VMEM((rows, n), bf16),
             VMEM((rows, LANES), f32), dma((3,)), dma],
            (grad_parts, values, row_scale, late[0], step_size, new_weights), 8 * rows * n, {5: 0},
        )
        start += n
    for blocks, values in zip(LATE, late):
        n = blocks * BLOCK
        (new_weights,) = call(
            functools.partial(place_kernel, start, width), [HBM, HBM], [(HBM, out_shape)],
            [VMEM((rows, n), bf16), dma((2,))], (values, new_weights), 4 * rows * n, {1: 0},
        )
        start += n
    return (
        new_params, new_weights, new_rows.reshape(rows), new_cols.reshape(width), update,
        clip_factor.reshape(()), param_scale.reshape(()),
    )


def solution(mesh):
    in_specs = (P("row", ("col", "dp")), P("dp", "row", "col"), P("row"), P("col"))
    out_specs = (
        P("row", ("col", "dp")),
        P("row", "col"),
        P("row"),
        P(("col", "dp")),
        P("row", ("col", "dp")),
        P(),
        P(),
    )
    return jax.shard_map(shards, mesh=mesh, in_specs=in_specs, out_specs=out_specs, check_vma=False)
```

```python
import functools

import jax
import jax.numpy as jnp
from jax import lax
from jax.experimental import pallas as pl
from jax.experimental.pallas import tpu as pltpu
from jax.sharding import PartitionSpec as P

R = 2048
C = 36864
STEP = 10
DECAY = 1.0 - STEP ** (-0.8)
RELATIVE = min(0.01, STEP ** (-0.5))
LANES = 128
SWAP = [(0, 1), (1, 0)]
BLOCK = 512
WIDE = 1536
AHEAD = (3, 2)
EARLY = sum(AHEAD)
SCALES = 2 * AHEAD[1] * BLOCK
LATE = (2, 2)
VMEM_LIMIT = 24 << 20
HALF_LIMIT = 24 << 20
MOMENTS_LIMIT = 24 << 20
WEIGHTS_LIMIT = 24 << 20
f32, bf16 = jnp.float32, jnp.bfloat16
shape = jax.ShapeDtypeStruct


def down(row):
    return jnp.broadcast_to(row, (LANES, LANES)).T


def flat(acc):
    return jnp.sum(acc.T, axis=0, keepdims=True)


def tile(at):
    return slice(at * LANES, (at + 1) * LANES)


def span(start, count):
    return pl.ds(pl.multiple_of(start, LANES), count)


def begin(*copies):
    copies = [pltpu.make_async_copy(*copy) for copy in copies]
    for copy in copies:
        copy.start()
    return copies


def steps(width):
    return [(start, WIDE) for start in range(0, width, WIDE)]


def half_kernel(grad_ref, out_ref, buf, in_sems, out_sems):
    width = buf.shape[1]
    other = (1 - lax.axis_index("dp")) * width
    pieces = steps(width)
    ins = [
        begin((grad_ref.at[0, :, span(other + s, n)], buf.at[:, s : s + n], in_sems.at[i]))[0]
        for i, (s, n) in enumerate(pieces)
    ]
    outs = []
    for i, (s, n) in enumerate(pieces):
        ins[i].wait()
        outs += begin((buf.at[:, s : s + n], out_ref.at[:, s : s + n], out_sems.at[i]))
    for copy in outs:
        copy.wait()


def prepare_kernel(grad_ref, params_ref, _, *refs):
    ahead_refs, (weight_ref, params, parts, values, sems, out_sems) = refs[: len(AHEAD)], refs[len(AHEAD) :]
    width = params.shape[1]
    mine = lax.axis_index("dp") * width
    pieces = steps(width)
    ins = [
        begin((params_ref.at[:, s : s + n], params.at[:, s : s + n], sems.at[i]))[0] for i, (s, n) in enumerate(pieces)
    ]
    grad = begin((grad_ref.at[0, :, span(mine, EARLY * BLOCK)], parts, sems.at[len(pieces)]))[0]
    acc = jnp.zeros((LANES, LANES), f32)
    for i, (s, n) in enumerate(pieces):
        ins[i].wait()
        for t in range(s // LANES, (s + n) // LANES):
            value = params[:, tile(t)]
            acc = acc + value * value
            if t < EARLY * BLOCK // LANES:
                values[:, tile(t)] = value.astype(bf16)
    grad.wait()
    outs, start = [], 0
    for i, (count, ahead_ref) in enumerate(zip(AHEAD, ahead_refs)):
        n = count * BLOCK
        outs += begin(
            (parts.at[:, start : start + n], ahead_ref.at[:, 0:n], out_sems.at[2 * i]),
            (values.at[:, start : start + n], ahead_ref.at[:, n : 2 * n], out_sems.at[2 * i + 1]),
        )
        start += n
    weight_ref[...] = jnp.sum(jnp.sum(acc, axis=0, keepdims=True), axis=1, keepdims=True)
    for copy in outs:
        copy.wait()


def sums_kernel(grad_parts_ref, got_ref, _, grad_ref, row_ref, sent_ref, mine, got, grad, cols, sems, out_sems):
    width = grad.shape[1]
    first = lax.axis_index("dp") * width
    pieces = steps(width)
    ins = [
        begin(
            (grad_parts_ref.at[0, :, span(first + s, n)], mine.at[:, s : s + n], sems.at[2 * i]),
            (got_ref.at[:, s : s + n], got.at[:, s : s + n], sems.at[2 * i + 1]),
        )
        for i, (s, n) in enumerate(pieces)
    ]
    cols[...] = jnp.zeros_like(cols)
    acc = jnp.zeros((LANES, LANES), f32)
    outs = []
    for i, (s, n) in enumerate(pieces):
        for copy in ins[i]:
            copy.wait()
        for t in range(s // LANES, (s + n) // LANES):
            g = mine[:, tile(t)].astype(f32) + got[:, tile(t)].astype(f32)
            grad[:, tile(t)] = g
            squares = g * g + 1e-30
            acc = acc + squares
            cols[t : t + 1, :] = jnp.sum(squares, axis=0, keepdims=True)
        outs += begin((grad.at[:, s : s + n], grad_ref.at[:, s : s + n], out_sems.at[i]))
    row_ref[...] = flat(acc)
    sent = cols[...].astype(bf16)
    for peer in range(sent_ref.shape[0]):
        sent_ref[peer] = sent
    for copy in outs:
        copy.wait()


def moments_kernel(
    grad_ref, got_ref, row_ref, old_rows_ref, old_cols_ref, weight_ref, _,
    new_cols_ref, copy_ref, sent_ref, ahead_ref, grad, inv_cols, sent, scale, rounded, sems, out_sems,
):
    width = grad.shape[1]
    height = width // LANES
    pieces = steps(width)
    ins = [begin((grad_ref.at[:, s : s + n], grad.at[:, s : s + n], sems.at[i]))[0] for i, (s, n) in enumerate(pieces)]
    totals = got_ref[0].astype(f32)
    for peer in range(1, got_ref.shape[0]):
        totals = totals + got_ref[peer].astype(f32)
    old_cols = jnp.where(lax.axis_index("dp") == 0, old_cols_ref[:height], old_cols_ref[height:])
    new_cols = DECAY * old_cols + (1.0 - DECAY) * (totals[:height] / R)
    new_cols_ref[...] = new_cols
    copy_ref[...] = new_cols
    inv_cols[...] = 1.0 / new_cols
    scale[...] = jnp.zeros_like(scale)
    scale[: EARLY * BLOCK // LANES] = lax.rsqrt(new_cols[: EARLY * BLOCK // LANES])
    rounded[...] = scale[...].astype(bf16)
    (scale_copy,) = begin((rounded, ahead_ref.at[:, SCALES : SCALES + LANES], out_sems.at[0]))
    acc = jnp.zeros((LANES, LANES), f32)
    for i, (s, n) in enumerate(pieces):
        ins[i].wait()
        for t in range(s // LANES, (s + n) // LANES):
            g = grad[:, tile(t)]
            acc = acc + g * g * inv_cols[t : t + 1, :]
    at = lax.broadcasted_iota(jnp.int32, (4, LANES), 0)
    value = jnp.zeros((4, LANES), f32)
    for i, row in enumerate([row_ref[...], flat(acc), old_rows_ref[...], weight_ref[...]]):
        value = jnp.where(at == i, jnp.broadcast_to(row, (4, LANES)), value)
    sent[...] = jnp.broadcast_to(value[None], sent.shape)
    (copy,) = begin((sent, sent_ref, out_sems.at[1]))
    scale_copy.wait()
    copy.wait()


def weights_piece(grad, params, out_ref, row_scale, col_scale, step_size, first):
    for t in range(grad.shape[1] // LANES):
        update = grad[:, tile(t)] * row_scale * col_scale[first + t : first + t + 1, :]
        out_ref[:, tile(t)] = (params[:, tile(t)] - step_size * update).astype(bf16)


def first_weights_kernel(
    got_ref, cols_ref, grad_ref, params_ref,
    out_ref, rows_ref, clip_ref, scale_ref, step_ref, row_scale, col_scale, grad, params, all_rows, sems,
):
    start, count = EARLY * BLOCK, grad.shape[1]
    ins = begin(
        (grad_ref.at[:, start : start + count], grad, sems.at[0]),
        (params_ref.at[:, start : start + count], params, sems.at[1]),
    )
    update_sum = jnp.zeros((1, LANES), f32)
    row_sum = jnp.zeros((1, LANES), f32)
    weight_sum = jnp.zeros((1, LANES), f32)
    for block in range(16):
        got = None
        for d in range(2):
            for c in range(4):
                term = got_ref[d * 64 + block * 4 + c]
                got = term if got is None else got + term
        rows = DECAY * got_ref[block * 4][2:3] + (1.0 - DECAY) * (got[0:1] / C)
        all_rows[block : block + 1, :] = rows
        update_sum = update_sum + got[1:2] / rows
        row_sum = row_sum + rows
        weight_sum = weight_sum + got[3:4]
    row_mean = jnp.sum(row_sum, axis=1, keepdims=True) / R
    rows = all_rows[pl.ds(lax.axis_index("row"), 1), :]
    rows_ref[...] = rows
    row_scale[...] = down(lax.rsqrt(rows / row_mean))
    col_scale[...] = lax.rsqrt(cols_ref[...])
    update_mean = jnp.sum(update_sum, axis=1, keepdims=True) * row_mean / (R * C)
    weight_mean = weight_sum[:, :1] / (R * C)
    clip_factor = jnp.maximum(1.0, jnp.sqrt(update_mean))
    param_scale = jnp.maximum(0.001, jnp.sqrt(weight_mean))
    clip_ref[...] = clip_factor
    scale_ref[...] = param_scale
    step_size = RELATIVE * param_scale / clip_factor
    step_ref[...] = step_size
    for copy in ins:
        copy.wait()
    weights_piece(grad, params, out_ref, row_scale[...], col_scale, step_size, start // LANES)


def weights_kernel(start, grad_ref, params_ref, row_scale, col_scale, step_ref, out_ref, grad, params, sems):
    count = grad.shape[1]
    ins = begin(
        (grad_ref.at[:, start : start + count], grad, sems.at[0]),
        (params_ref.at[:, start : start + count], params, sems.at[1]),
    )
    for copy in ins:
        copy.wait()
    weights_piece(grad, params, out_ref, row_scale[...], col_scale, step_ref[...], start // LANES)


def params_kernel(
    grad_ref, params_ref, row_scale, col_scale, step_ref,
    new_ref, update_ref, weights_ref, grad, params, update, new, weights, sems, out_sems,
):
    width = grad.shape[1]
    mine = lax.axis_index("dp") * width
    pieces = steps(width)
    ins = [
        begin(
            (grad_ref.at[:, s : s + n], grad.at[:, s : s + n], sems.at[2 * i]),
            (params_ref.at[:, s : s + n], params.at[:, s : s + n], sems.at[2 * i + 1]),
        )
        for i, (s, n) in enumerate(pieces)
    ]
    across, step_size = row_scale[...], step_ref[...]
    outs = []
    for i, (s, n) in enumerate(pieces):
        for copy in ins[i]:
            copy.wait()
        for t in range(s // LANES, (s + n) // LANES):
            value = grad[:, tile(t)] * across * col_scale[t : t + 1, :]
            moved = params[:, tile(t)] - step_size * value
            update[:, tile(t)] = value
            new[:, tile(t)] = moved
            weights[:, tile(t)] = moved.astype(bf16)
        outs += begin(
            (update.at[:, s : s + n], update_ref.at[:, s : s + n], out_sems.at[3 * i]),
            (new.at[:, s : s + n], new_ref.at[:, s : s + n], out_sems.at[3 * i + 1]),
            (weights.at[:, s : s + n], weights_ref.at[:, span(mine + s, n)], out_sems.at[3 * i + 2]),
        )
    for copy in outs:
        copy.wait()


def early_kernel(start, width, grad_ref, ahead_ref, row_scale, scale_ref, step_ref, _, out_ref,
                 mine, got, scale, out, scales, sems, out_sem):
    count = mine.shape[1]
    first = (1 - lax.axis_index("dp")) * width + start
    ins = begin(
        (scale_ref.at[:, SCALES : SCALES + LANES], scale, sems.at[0]),
        (grad_ref.at[0, :, span(first, count)], mine, sems.at[1]),
        (ahead_ref.at[:, 0 : 2 * count], got, sems.at[2]),
    )
    across, step_size = row_scale[...], step_ref[...]
    for copy in ins:
        copy.wait()
    scales[...] = scale[...].astype(f32)
    for t in range(count // LANES):
        g = mine[:, tile(t)].astype(f32) + got[:, tile(t)].astype(f32)
        at = start // LANES + t
        update = g * across * scales[at : at + 1, :]
        out[:, tile(t)] = (got[:, tile(count // LANES + t)].astype(f32) - step_size * update).astype(bf16)
    (copy,) = begin((out, out_ref.at[:, span(first, count)], out_sem))
    copy.wait()


def place_kernel(start, width, got_ref, _, out_ref, got, sems):
    first = (1 - lax.axis_index("dp")) * width + start
    count = got.shape[1]
    (copy,) = begin((got_ref.at[:, 0:count], got, sems.at[0]))
    copy.wait()
    (copy,) = begin((got, out_ref.at[:, span(first, count)], sems.at[1]))
    copy.wait()


HBM, VMEM = pltpu.HBM, pltpu.VMEM
dma = pltpu.SemaphoreType.DMA


def call(kernel, ins, outs, scratch, args, nbytes, aliases=None, limit=VMEM_LIMIT):
    return pl.pallas_call(
        kernel,
        in_specs=[pl.BlockSpec(memory_space=space) for space in ins],
        out_specs=[pl.BlockSpec(memory_space=space) for space, _ in outs],
        out_shape=[out for _, out in outs],
        scratch_shapes=list(scratch),
        input_output_aliases=aliases or {},
        cost_estimate=pl.CostEstimate(flops=nbytes, bytes_accessed=nbytes, transcendentals=0),
        compiler_params=pltpu.CompilerParams(vmem_limit_bytes=limit),
    )(*args)


def shards(params, grad_parts, row_moment, col_moment):
    rows, width = params.shape
    height = width // LANES
    padded = -(-height // 16) * 16
    early = EARLY * BLOCK
    count = len(steps(width))

    (outgoing,) = call(
        half_kernel, [HBM], [(HBM, shape((rows, width), bf16))],
        [VMEM((rows, width), bf16), dma((count,)), dma((count,))], (grad_parts,), 4 * rows * width, None, HALF_LIMIT,
    )
    got = lax.ppermute(outgoing, "dp", SWAP)
    *ahead, weight_part = call(
        prepare_kernel, [HBM, HBM, HBM],
        [(HBM, shape((rows, 2 * n * BLOCK + extra), bf16)) for n, extra in zip(AHEAD, (0, LANES))] + [(VMEM, shape((1, 1), f32))],
        [VMEM((rows, width), f32), VMEM((rows, early), bf16), VMEM((rows, early), bf16), dma((count + 1,)),
         dma((2 * len(AHEAD),))],
        (grad_parts, params, outgoing), 4 * rows * (width + early),
    )
    arrived = [lax.ppermute(ahead[0], "dp", SWAP)]

    gradient, row_part, sent = call(
        sums_kernel, [HBM, HBM, VMEM],
        [(HBM, shape((rows, width), f32)), (VMEM, shape((1, rows), f32)),
         (VMEM, shape((16, padded, LANES), bf16))],
        [VMEM((rows, width), bf16), VMEM((rows, width), bf16), VMEM((rows, width), f32), VMEM((padded, LANES), f32),
         dma((2 * count,)), dma((count,))],
        (grad_parts, got, weight_part), 8 * rows * width,
    )
    col_parts = lax.all_to_all(sent, "row", 0, 0)
    new_cols, cols_copy, sent, second = call(
        moments_kernel, [HBM] + [VMEM] * 5 + [HBM],
        [(VMEM, shape((height, LANES), f32)), (VMEM, shape((height, LANES), f32)),
         (HBM, shape((128, 4, LANES), f32)), (HBM, ahead[1])],
        [VMEM((rows, width), f32), VMEM((height, LANES), f32), VMEM((128, 4, LANES), f32), VMEM((rows, LANES), f32),
         VMEM((rows, LANES), bf16), dma((count,)), dma((2,))],
        (gradient, col_parts, row_part, row_moment.reshape(1, rows), col_moment.reshape(2 * height, LANES), weight_part,
         ahead[1]),
        4 * rows * width, {6: 3}, MOMENTS_LIMIT,
    )
    sent, arrived[0], second = lax.optimization_barrier((sent, arrived[0], second))
    parts = lax.all_to_all(sent, ("dp", "row", "col"), 0, 0)
    arrived.append(lax.ppermute(second, "dp", SWAP))

    n = LATE[0] * BLOCK
    out, new_rows, clip_factor, param_scale, step_size, row_scale, col_scale = call(
        first_weights_kernel, [VMEM, VMEM, HBM, HBM],
        [(VMEM, shape((rows, n), bf16)), (VMEM, shape((1, rows), f32)),
         (VMEM, shape((1, 1), f32)), (VMEM, shape((1, 1), f32)), (VMEM, shape((1, 1), f32)),
         (VMEM, shape((rows, LANES), f32)), (VMEM, shape((height, LANES), f32))],
        [VMEM((rows, n), f32), VMEM((rows, n), f32), VMEM((16, LANES), f32), dma((2,))],
        (parts, cols_copy, gradient, params), 8 * rows * n, None, WEIGHTS_LIMIT,
    )
    late = [lax.ppermute(out, "dp", SWAP)]
    start = early + n
    for blocks in LATE[1:]:
        n = blocks * BLOCK
        (out,) = call(
            functools.partial(weights_kernel, start), [HBM, HBM, VMEM, VMEM, VMEM],
            [(VMEM, shape((rows, n), bf16))], [VMEM((rows, n), f32), VMEM((rows, n), f32), dma((2,))],
            (gradient, params, row_scale, col_scale, step_size), 8 * rows * n,
        )
        late.append(lax.ppermute(out, "dp", SWAP))
        start += n

    out_shape = shape((rows, 2 * width), bf16)
    new_params, update, new_weights = call(
        params_kernel, [HBM, HBM, VMEM, VMEM, VMEM],
        [(HBM, shape((rows, width), f32)), (HBM, shape((rows, width), f32)), (HBM, out_shape)],
        [VMEM((rows, width), f32)] * 4 + [VMEM((rows, width), bf16), dma((2 * count,)), dma((3 * count,))],
        (gradient, params, row_scale, col_scale, step_size), 18 * rows * width,
    )
    start = 0
    for blocks, values in zip(AHEAD, arrived):
        n = blocks * BLOCK
        (new_weights,) = call(
            functools.partial(early_kernel, start, width), [HBM, HBM, VMEM, HBM, VMEM, HBM], [(HBM, out_shape)],
            [VMEM((rows, n), bf16), VMEM((rows, 2 * n), bf16), VMEM((rows, LANES), bf16), VMEM((rows, n), bf16),
             VMEM((rows, LANES), f32), dma((3,)), dma],
            (grad_parts, values, row_scale, arrived[1], step_size, new_weights), 8 * rows * n, {5: 0},
        )
        start += n
    for blocks, values in zip(LATE, late):
        n = blocks * BLOCK
        (new_weights,) = call(
            functools.partial(place_kernel, start, width), [HBM, HBM], [(HBM, out_shape)],
            [VMEM((rows, n), bf16), dma((2,))], (values, new_weights), 4 * rows * n, {1: 0},
        )
        start += n
    return (
        new_params, new_weights, new_rows.reshape(rows), new_cols.reshape(width), update,
        clip_factor.reshape(()), param_scale.reshape(()),
    )


def solution(mesh):
    in_specs = (P("row", ("col", "dp")), P("dp", "row", "col"), P("row"), P("col"))
    out_specs = (
        P("row", ("col", "dp")),
        P("row", "col"),
        P("row"),
        P(("col", "dp")),
        P("row", ("col", "dp")),
        P(),
        P(),
    )
    return jax.shard_map(shards, mesh=mesh, in_specs=in_specs, out_specs=out_specs, check_vma=False)
```

```python
import functools

import jax
import jax.numpy as jnp
from jax import lax
from jax.experimental import pallas as pl
from jax.experimental.pallas import tpu as pltpu
from jax.sharding import PartitionSpec as P

R = 2048
C = 36864
STEP = 10
DECAY = 1.0 - STEP ** (-0.8)
RELATIVE = min(0.01, STEP ** (-0.5))
LANES = 128
SWAP = [(0, 1), (1, 0)]
BLOCK = 256
WIDE = 1536
EARLY = 11
LATE = (4, 3)
VMEM_LIMIT = 24 << 20
f32, bf16 = jnp.float32, jnp.bfloat16
shape = jax.ShapeDtypeStruct


def down(row):
    return jnp.broadcast_to(row, (LANES, LANES)).T


def flat(acc):
    return jnp.sum(acc.T, axis=0, keepdims=True)


def split(value, count):
    parts = []
    for _ in range(count):
        parts.append(value.astype(bf16).astype(f32))
        value = value - parts[-1]
    return parts


def tile(at):
    return slice(at * LANES, (at + 1) * LANES)


def span(start, count):
    return pl.ds(pl.multiple_of(start, LANES), count)


def begin(*copies):
    copies = [pltpu.make_async_copy(*copy) for copy in copies]
    for copy in copies:
        copy.start()
    return copies


def steps(width):
    return [(start, WIDE) for start in range(0, width, WIDE)]


def half_kernel(grad_ref, out_ref, buf, in_sems, out_sems):
    width = buf.shape[1]
    other = (1 - lax.axis_index("dp")) * width
    pieces = steps(width)
    ins = [
        begin((grad_ref.at[0, :, span(other + s, n)], buf.at[:, s : s + n], in_sems.at[i]))[0]
        for i, (s, n) in enumerate(pieces)
    ]
    outs = []
    for i, (s, n) in enumerate(pieces):
        ins[i].wait()
        outs += begin((buf.at[:, s : s + n], out_ref.at[:, s : s + n], out_sems.at[i]))
    for copy in outs:
        copy.wait()


def prepare_kernel(grad_ref, params_ref, _, ahead_ref, weight_ref, params, parts, values, sems, out_sems):
    width, early = params.shape[1], parts.shape[1]
    mine = lax.axis_index("dp") * width
    pieces = steps(width)
    grad = begin((grad_ref.at[0, :, span(mine, early)], parts, sems.at[len(pieces)]))[0]
    ins = [
        begin((params_ref.at[:, s : s + n], params.at[:, s : s + n], sems.at[i]))[0] for i, (s, n) in enumerate(pieces)
    ]
    acc = jnp.zeros((LANES, LANES), f32)
    for i, (s, n) in enumerate(pieces):
        ins[i].wait()
        for t in range(s // LANES, (s + n) // LANES):
            value = params[:, tile(t)]
            acc = acc + value * value
            if t < early // LANES:
                values[:, tile(t)] = value.astype(bf16)
    grad.wait()
    outs = begin(
        (parts, ahead_ref.at[:, 0:early], out_sems.at[0]), (values, ahead_ref.at[:, early : 2 * early], out_sems.at[1])
    )
    weight_ref[...] = jnp.sum(jnp.sum(acc, axis=0, keepdims=True), axis=1, keepdims=True)
    for copy in outs:
        copy.wait()


def sums_kernel(grad_parts_ref, got_ref, old_rows_ref, _, grad_ref, row_ref, sent_ref, mine, got, grad, cols, sems, out_sems):
    width = grad.shape[1]
    first = lax.axis_index("dp") * width
    pieces = steps(width)
    ins = [
        begin(
            (grad_parts_ref.at[0, :, span(first + s, n)], mine.at[:, s : s + n], sems.at[2 * i]),
            (got_ref.at[:, s : s + n], got.at[:, s : s + n], sems.at[2 * i + 1]),
        )
        for i, (s, n) in enumerate(pieces)
    ]
    cols[...] = jnp.zeros_like(cols)
    acc = jnp.zeros((LANES, LANES), f32)
    outs = []
    for i, (s, n) in enumerate(pieces):
        for copy in ins[i]:
            copy.wait()
        for t in range(s // LANES, (s + n) // LANES):
            g = mine[:, tile(t)].astype(f32) + got[:, tile(t)].astype(f32)
            grad[:, tile(t)] = g
            squares = g * g + 1e-30
            acc = acc + squares
            cols[t : t + 1, :] = jnp.sum(squares, axis=0, keepdims=True)
        outs += begin((grad.at[:, s : s + n], grad_ref.at[:, s : s + n], out_sems.at[i]))
    row_ref[...] = flat(acc)
    for i, part in enumerate(split(old_rows_ref[...], 2)):
        cols[width // LANES + i : width // LANES + i + 1, :] = part
    sent = cols[...].astype(bf16)
    for peer in range(sent_ref.shape[0]):
        sent_ref[peer] = sent
    for copy in outs:
        copy.wait()


def moments_kernel(
    grad_ref, got_ref, row_ref, old_cols_ref, weight_ref,
    new_cols_ref, copy_ref, old_rows_ref, sent_ref, grad, inv_cols, sems,
):
    width = grad.shape[1]
    height = width // LANES
    pieces = steps(width)
    ins = [begin((grad_ref.at[:, s : s + n], grad.at[:, s : s + n], sems.at[i]))[0] for i, (s, n) in enumerate(pieces)]
    totals = got_ref[0].astype(f32)
    for peer in range(1, got_ref.shape[0]):
        totals = totals + got_ref[peer].astype(f32)
    for peer in range(got_ref.shape[0]):
        rows = got_ref[peer].astype(f32)
        old_rows_ref[peer : peer + 1, :] = rows[height : height + 1] + rows[height + 1 : height + 2]
    old_cols = jnp.where(lax.axis_index("dp") == 0, old_cols_ref[:height], old_cols_ref[height:])
    new_cols = DECAY * old_cols + (1.0 - DECAY) * (totals[:height] / R)
    new_cols_ref[...] = new_cols
    copy_ref[...] = new_cols
    inv_cols[...] = 1.0 / new_cols
    acc = jnp.zeros((LANES, LANES), f32)
    for i, (s, n) in enumerate(pieces):
        ins[i].wait()
        for t in range(s // LANES, (s + n) // LANES):
            g = grad[:, tile(t)]
            acc = acc + g * g * inv_cols[t : t + 1, :]
    lane = lax.broadcasted_iota(jnp.int32, (1, LANES), 1)
    weight = jnp.zeros((1, LANES), f32)
    for i, part in enumerate(split(jnp.broadcast_to(weight_ref[...], (1, LANES)), 3)):
        weight = jnp.where(lane == i, part, weight)
    at = lax.broadcasted_iota(jnp.int32, (4, LANES), 0)
    value = jnp.zeros((4, LANES), f32)
    for i, row in enumerate(split(row_ref[...], 2) + [flat(acc), weight]):
        value = jnp.where(at == i, jnp.broadcast_to(row, (4, LANES)), value)
    value = value.astype(bf16)
    sent_ref[...] = jnp.broadcast_to(value[None], sent_ref.shape)


def weights_piece(grad, params, out_ref, row_scale, col_scale, step_size, first):
    for t in range(grad.shape[1] // LANES):
        update = grad[:, tile(t)] * row_scale * col_scale[first + t : first + t + 1, :]
        out_ref[:, tile(t)] = (params[:, tile(t)] - step_size * update).astype(bf16)


def first_weights_kernel(
    got_ref, cols_ref, old_rows_ref, grad_ref, params_ref,
    out_ref, rows_ref, clip_ref, scale_ref, step_ref, row_scale, col_scale, grad, params, all_rows, scale, sems,
):
    start, count = EARLY * BLOCK, grad.shape[1]
    ins = begin(
        (grad_ref.at[:, start : start + count], grad, sems.at[0]),
        (params_ref.at[:, start : start + count], params, sems.at[1]),
    )
    update_sum = jnp.zeros((1, LANES), f32)
    row_sum = jnp.zeros((1, LANES), f32)
    weight_sum = jnp.zeros((1, LANES), f32)
    for block in range(16):
        got = None
        for d in range(2):
            for c in range(4):
                term = got_ref[d * 64 + block * 4 + c].astype(f32)
                got = term if got is None else got + term
        rows = DECAY * old_rows_ref[block : block + 1, :] + (1.0 - DECAY) * ((got[0:1] + got[1:2]) / C)
        all_rows[block : block + 1, :] = rows
        update_sum = update_sum + got[2:3] / rows
        row_sum = row_sum + rows
        weight_sum = weight_sum + got[3:4]
    row_mean = jnp.sum(row_sum, axis=1, keepdims=True) / R
    rows = all_rows[pl.ds(lax.axis_index("row"), 1), :]
    rows_ref[...] = rows
    row_scale[...] = down(lax.rsqrt(rows / row_mean))
    col_scale[...] = lax.rsqrt(cols_ref[...])
    update_mean = jnp.sum(update_sum, axis=1, keepdims=True) * row_mean / (R * C)
    weight_mean = jnp.sum(weight_sum, axis=1, keepdims=True) / (R * C)
    clip_factor = jnp.maximum(1.0, jnp.sqrt(update_mean))
    param_scale = jnp.maximum(0.001, jnp.sqrt(weight_mean))
    clip_ref[...] = clip_factor
    scale_ref[...] = param_scale
    step_size = RELATIVE * param_scale / clip_factor
    step_ref[...] = step_size
    scale[...] = jnp.zeros_like(scale)
    scale[: start // LANES] = col_scale[: start // LANES]
    out_ref[:, count : count + LANES] = scale[...].astype(bf16)
    for copy in ins:
        copy.wait()
    weights_piece(grad, params, out_ref, row_scale[...], col_scale, step_size, start // LANES)


def weights_kernel(start, grad_ref, params_ref, row_scale, col_scale, step_ref, out_ref, grad, params, sems):
    count = grad.shape[1]
    ins = begin(
        (grad_ref.at[:, start : start + count], grad, sems.at[0]),
        (params_ref.at[:, start : start + count], params, sems.at[1]),
    )
    for copy in ins:
        copy.wait()
    weights_piece(grad, params, out_ref, row_scale[...], col_scale, step_ref[...], start // LANES)


def params_kernel(
    grad_ref, params_ref, row_scale, col_scale, step_ref,
    new_ref, update_ref, weights_ref, grad, params, update, new, weights, sems, out_sems,
):
    width = grad.shape[1]
    mine = lax.axis_index("dp") * width
    pieces = steps(width)
    ins = [
        begin(
            (grad_ref.at[:, s : s + n], grad.at[:, s : s + n], sems.at[2 * i]),
            (params_ref.at[:, s : s + n], params.at[:, s : s + n], sems.at[2 * i + 1]),
        )
        for i, (s, n) in enumerate(pieces)
    ]
    across, step_size = row_scale[...], step_ref[...]
    outs = []
    for i, (s, n) in enumerate(pieces):
        for copy in ins[i]:
            copy.wait()
        for t in range(s // LANES, (s + n) // LANES):
            value = grad[:, tile(t)] * across * col_scale[t : t + 1, :]
            moved = params[:, tile(t)] - step_size * value
            update[:, tile(t)] = value
            new[:, tile(t)] = moved
            weights[:, tile(t)] = moved.astype(bf16)
        outs += begin(
            (update.at[:, s : s + n], update_ref.at[:, s : s + n], out_sems.at[3 * i]),
            (new.at[:, s : s + n], new_ref.at[:, s : s + n], out_sems.at[3 * i + 1]),
            (weights.at[:, s : s + n], weights_ref.at[:, span(mine + s, n)], out_sems.at[3 * i + 2]),
        )
    for copy in outs:
        copy.wait()


def early_kernel(width, grad_ref, ahead_ref, row_scale, late_ref, step_ref, _, out_ref,
                 mine, got, late, out, scale, sems, out_sems):
    count, extra = mine.shape[1], late.shape[1] - LANES
    first = (1 - lax.axis_index("dp")) * width
    ins = begin(
        (grad_ref.at[0, :, span(first, count)], mine, sems.at[0]),
        (ahead_ref, got, sems.at[1]),
        (late_ref, late, sems.at[2]),
    )
    across, step_size = row_scale[...], step_ref[...]
    ins[2].wait()
    outs = begin((late.at[:, 0:extra], out_ref.at[:, span(first + count, extra)], out_sems.at[0]))
    scale[...] = late[:, extra : extra + LANES].astype(f32)
    for copy in ins[:2]:
        copy.wait()
    for t in range(count // LANES):
        g = mine[:, tile(t)].astype(f32) + got[:, tile(t)].astype(f32)
        update = g * across * scale[t : t + 1, :]
        out[:, tile(t)] = (got[:, tile(count // LANES + t)].astype(f32) - step_size * update).astype(bf16)
    outs += begin((out, out_ref.at[:, span(first, count)], out_sems.at[1]))
    for copy in outs:
        copy.wait()


def place_kernel(start, width, got_ref, _, out_ref, got, sems):
    first = (1 - lax.axis_index("dp")) * width + start
    count = got.shape[1]
    (copy,) = begin((got_ref.at[:, 0:count], got, sems.at[0]))
    copy.wait()
    (copy,) = begin((got, out_ref.at[:, span(first, count)], sems.at[1]))
    copy.wait()


HBM, VMEM = pltpu.HBM, pltpu.VMEM
dma = pltpu.SemaphoreType.DMA


def call(kernel, ins, outs, scratch, args, nbytes, aliases=None, limit=VMEM_LIMIT):
    return pl.pallas_call(
        kernel,
        in_specs=[pl.BlockSpec(memory_space=space) for space in ins],
        out_specs=[pl.BlockSpec(memory_space=space) for space, _ in outs],
        out_shape=[out for _, out in outs],
        scratch_shapes=list(scratch),
        input_output_aliases=aliases or {},
        cost_estimate=pl.CostEstimate(flops=nbytes, bytes_accessed=nbytes, transcendentals=0),
        compiler_params=pltpu.CompilerParams(vmem_limit_bytes=limit),
    )(*args)


def shards(params, grad_parts, row_moment, col_moment):
    rows, width = params.shape
    height = width // LANES
    padded = -(-height // 16) * 16
    early = EARLY * BLOCK
    count = len(steps(width))

    (outgoing,) = call(
        half_kernel, [HBM], [(HBM, shape((rows, width), bf16))],
        [VMEM((rows, width), bf16), dma((count,)), dma((count,))], (grad_parts,), 4 * rows * width,
    )
    got = lax.ppermute(outgoing, "dp", SWAP)
    ahead, weight_part = call(
        prepare_kernel, [HBM, HBM, HBM],
        [(HBM, shape((rows, 2 * early), bf16)), (VMEM, shape((1, 1), f32))],
        [VMEM((rows, width), f32), VMEM((rows, early), bf16), VMEM((rows, early), bf16), dma((count + 1,)), dma((2,))],
        (grad_parts, params, outgoing), 4 * rows * (width + early),
    )
    ahead = lax.ppermute(ahead, "dp", SWAP)

    gradient, row_part, sent = call(
        sums_kernel, [HBM, HBM, VMEM, VMEM],
        [(HBM, shape((rows, width), f32)), (VMEM, shape((1, rows), f32)),
         (VMEM, shape((16, padded, LANES), bf16))],
        [VMEM((rows, width), bf16), VMEM((rows, width), bf16), VMEM((rows, width), f32), VMEM((padded, LANES), f32),
         dma((2 * count,)), dma((count,))],
        (grad_parts, got, row_moment.reshape(1, rows), weight_part), 8 * rows * width,
    )
    col_parts = lax.all_to_all(sent, "row", 0, 0)
    new_cols, cols_copy, old_rows, sent = call(
        moments_kernel, [HBM] + [VMEM] * 4,
        [(VMEM, shape((height, LANES), f32)), (VMEM, shape((height, LANES), f32)),
         (VMEM, shape((16, LANES), f32)), (VMEM, shape((128, 4, LANES), bf16))],
        [VMEM((rows, width), f32), VMEM((height, LANES), f32), dma((count,))],
        (gradient, col_parts, row_part, col_moment.reshape(2 * height, LANES), weight_part),
        4 * rows * width,
    )
    parts = lax.all_to_all(sent, ("dp", "row", "col"), 0, 0)

    n = LATE[0] * BLOCK
    out, new_rows, clip_factor, param_scale, step_size, row_scale, col_scale = call(
        first_weights_kernel, [VMEM, VMEM, VMEM, HBM, HBM],
        [(VMEM, shape((rows, n + LANES), bf16)), (VMEM, shape((1, rows), f32)),
         (VMEM, shape((1, 1), f32)), (VMEM, shape((1, 1), f32)), (VMEM, shape((1, 1), f32)),
         (VMEM, shape((rows, LANES), f32)), (VMEM, shape((height, LANES), f32))],
        [VMEM((rows, n), f32), VMEM((rows, n), f32), VMEM((16, LANES), f32), VMEM((rows, LANES), f32), dma((2,))],
        (parts, cols_copy, old_rows, gradient, params), 8 * rows * n,
    )
    late = [lax.ppermute(out, "dp", SWAP)]
    start = early + n
    for blocks in LATE[1:]:
        n = blocks * BLOCK
        (out,) = call(
            functools.partial(weights_kernel, start), [HBM, HBM, VMEM, VMEM, VMEM],
            [(VMEM, shape((rows, n), bf16))], [VMEM((rows, n), f32), VMEM((rows, n), f32), dma((2,))],
            (gradient, params, row_scale, col_scale, step_size), 8 * rows * n,
        )
        late.append(lax.ppermute(out, "dp", SWAP))
        start += n

    out_shape = shape((rows, 2 * width), bf16)
    new_params, update, new_weights = call(
        params_kernel, [HBM, HBM, VMEM, VMEM, VMEM],
        [(HBM, shape((rows, width), f32)), (HBM, shape((rows, width), f32)), (HBM, out_shape)],
        [VMEM((rows, width), f32)] * 4 + [VMEM((rows, width), bf16), dma((2 * count,)), dma((3 * count,))],
        (gradient, params, row_scale, col_scale, step_size), 18 * rows * width,
    )
    n = LATE[0] * BLOCK
    (new_weights,) = call(
        functools.partial(early_kernel, width), [HBM, HBM, VMEM, HBM, VMEM, HBM], [(HBM, out_shape)],
        [VMEM((rows, early), bf16), VMEM((rows, 2 * early), bf16), VMEM((rows, n + LANES), bf16),
         VMEM((rows, early), bf16), VMEM((rows, LANES), f32), dma((3,)), dma((2,))],
        (grad_parts, ahead, row_scale, late[0], step_size, new_weights), 8 * rows * early, {5: 0},
    )
    start = early + n
    for blocks, values in zip(LATE[1:], late[1:]):
        n = blocks * BLOCK
        (new_weights,) = call(
            functools.partial(place_kernel, start, width), [HBM, HBM], [(HBM, out_shape)],
            [VMEM((rows, n), bf16), dma((2,))], (values, new_weights), 4 * rows * n, {1: 0},
        )
        start += n
    return (
        new_params, new_weights, new_rows.reshape(rows), new_cols.reshape(width), update,
        clip_factor.reshape(()), param_scale.reshape(()),
    )


def solution(mesh):
    in_specs = (P("row", ("col", "dp")), P("dp", "row", "col"), P("row"), P("col"))
    out_specs = (
        P("row", ("col", "dp")),
        P("row", "col"),
        P("row"),
        P(("col", "dp")),
        P("row", ("col", "dp")),
        P(),
        P(),
    )
    return jax.shard_map(shards, mesh=mesh, in_specs=in_specs, out_specs=out_specs, check_vma=False)
```

```python
import functools

import jax
import jax.numpy as jnp
from jax import lax
from jax.experimental import pallas as pl
from jax.experimental.pallas import tpu as pltpu
from jax.sharding import PartitionSpec as P

R = 2048
C = 36864
STEP = 10
DECAY = 1.0 - STEP ** (-0.8)
RELATIVE = min(0.01, STEP ** (-0.5))
LANES = 128
SWAP = [(0, 1), (1, 0)]
BLOCK = 256
WIDE = 1536
EARLY = 11
LATE = (7,)
VMEM_LIMIT = 24 << 20
f32, bf16 = jnp.float32, jnp.bfloat16
shape = jax.ShapeDtypeStruct


def down(row):
    return jnp.broadcast_to(row, (LANES, LANES)).T


def flat(acc):
    return jnp.sum(acc.T, axis=0, keepdims=True)


def split(value, count):
    parts = []
    for _ in range(count):
        parts.append(value.astype(bf16).astype(f32))
        value = value - parts[-1]
    return parts


def lanes(value):
    at = lax.broadcasted_iota(jnp.int32, (1, LANES), 1)
    row = jnp.zeros((1, LANES), f32)
    for i, part in enumerate(split(jnp.broadcast_to(value, (1, LANES)), 3)):
        row = jnp.where(at == i, part, row)
    return row


def tile(at):
    return slice(at * LANES, (at + 1) * LANES)


def span(start, count):
    return pl.ds(pl.multiple_of(start, LANES), count)


def begin(*copies):
    copies = [pltpu.make_async_copy(*copy) for copy in copies]
    for copy in copies:
        copy.start()
    return copies


def steps(width):
    return [(start, WIDE) for start in range(0, width, WIDE)]


def half_kernel(grad_ref, out_ref, buf, in_sems, out_sems):
    width = buf.shape[1]
    other = (1 - lax.axis_index("dp")) * width
    pieces = steps(width)
    ins = [
        begin((grad_ref.at[0, :, span(other + s, n)], buf.at[:, s : s + n], in_sems.at[i]))[0]
        for i, (s, n) in enumerate(pieces)
    ]
    outs = []
    for i, (s, n) in enumerate(pieces):
        ins[i].wait()
        outs += begin((buf.at[:, s : s + n], out_ref.at[:, s : s + n], out_sems.at[i]))
    for copy in outs:
        copy.wait()


def prepare_kernel(grad_ref, params_ref, _, ahead_ref, weight_ref, params, parts, values, sems, out_sems):
    width, early = params.shape[1], parts.shape[1]
    mine = lax.axis_index("dp") * width
    pieces = steps(width)
    grad = begin((grad_ref.at[0, :, span(mine, early)], parts, sems.at[len(pieces)]))[0]
    ins = [
        begin((params_ref.at[:, s : s + n], params.at[:, s : s + n], sems.at[i]))[0] for i, (s, n) in enumerate(pieces)
    ]
    acc = jnp.zeros((LANES, LANES), f32)
    for i, (s, n) in enumerate(pieces):
        ins[i].wait()
        for t in range(s // LANES, (s + n) // LANES):
            value = params[:, tile(t)]
            acc = acc + value * value
            if t < early // LANES:
                values[:, tile(t)] = value.astype(bf16)
    grad.wait()
    outs = begin(
        (parts, ahead_ref.at[:, 0:early], out_sems.at[0]), (values, ahead_ref.at[:, early : 2 * early], out_sems.at[1])
    )
    weight_ref[...] = jnp.sum(jnp.sum(acc, axis=0, keepdims=True), axis=1, keepdims=True)
    for copy in outs:
        copy.wait()


def sums_kernel(grad_parts_ref, got, old_rows_ref, weight_ref, grad, row_ref, sent_ref, mine, cols, sems):
    width = grad.shape[1]
    first = lax.axis_index("dp") * width
    pieces = steps(width)
    ins = [
        begin((grad_parts_ref.at[0, :, span(first + s, n)], mine.at[:, s : s + n], sems.at[i]))[0]
        for i, (s, n) in enumerate(pieces)
    ]
    cols[...] = jnp.zeros_like(cols)
    acc = jnp.zeros((LANES, LANES), f32)
    for i, (s, n) in enumerate(pieces):
        ins[i].wait()
        for t in range(s // LANES, (s + n) // LANES):
            g = mine[:, tile(t)].astype(f32) + got[:, tile(t)].astype(f32)
            grad[:, tile(t)] = g
            squares = g * g + 1e-30
            acc = acc + squares
            cols[t : t + 1, :] = jnp.sum(squares, axis=0, keepdims=True)
    row_ref[...] = flat(acc)
    free = width // LANES
    for i, part in enumerate(split(old_rows_ref[...], 2) + [lanes(weight_ref[...])]):
        cols[free + i : free + i + 1, :] = part
    sent = cols[...].astype(bf16)
    for peer in range(sent_ref.shape[0]):
        sent_ref[peer] = sent


def moments_kernel(
    grad, got_ref, row_ref, old_cols_ref, new_cols_ref, copy_ref, old_rows_ref, sent_ref, inv_cols, scale,
):
    height = grad.shape[1] // LANES
    totals = got_ref[0].astype(f32)
    for peer in range(1, got_ref.shape[0]):
        totals = totals + got_ref[peer].astype(f32)
    for peer in range(got_ref.shape[0]):
        rows = got_ref[peer].astype(f32)
        old_rows_ref[peer : peer + 1, :] = rows[height : height + 1] + rows[height + 1 : height + 2]
    weight = jnp.sum(totals[height + 2 : height + 3], axis=1, keepdims=True)
    old_cols = jnp.where(lax.axis_index("dp") == 0, old_cols_ref[:height], old_cols_ref[height:])
    new_cols = DECAY * old_cols + (1.0 - DECAY) * (totals[:height] / R)
    new_cols_ref[...] = new_cols
    copy_ref[...] = new_cols
    inv_cols[...] = 1.0 / new_cols
    acc = jnp.zeros((LANES, LANES), f32)
    for t in range(height):
        g = grad[:, tile(t)]
        acc = acc + g * g * inv_cols[t : t + 1, :]
    scale[...] = lax.rsqrt(new_cols)
    index = lax.axis_index("row")
    second = jnp.where(index == 15, lanes(weight), scale[pl.ds(16 + index, 1), :])
    at = lax.broadcasted_iota(jnp.int32, (4, LANES), 0)
    value = jnp.zeros((4, LANES), f32)
    for i, row in enumerate([row_ref[...], flat(acc), scale[pl.ds(index, 1), :], second]):
        value = jnp.where(at == i, jnp.broadcast_to(row, (4, LANES)), value)
    value = value.astype(bf16)
    sent_ref[...] = jnp.broadcast_to(value[None], sent_ref.shape)


def weights_piece(grad, params, out_ref, row_scale, col_scale, step_size, first):
    for t in range(params.shape[1] // LANES):
        update = grad[:, tile(first + t)] * row_scale * col_scale[first + t : first + t + 1, :]
        out_ref[:, tile(t)] = (params[:, tile(t)] - step_size * update).astype(bf16)


def first_weights_kernel(
    got_ref, cols_ref, old_rows_ref, grad, params_ref,
    out_ref, rows_ref, clip_ref, scale_ref, step_ref, row_scale, col_scale, early_ref, params, all_rows, sem,
):
    start, count = EARLY * BLOCK, params.shape[1]
    (params_copy,) = begin((params_ref.at[:, start : start + count], params, sem))
    update_sum = jnp.zeros((1, LANES), f32)
    row_sum = jnp.zeros((1, LANES), f32)
    for block in range(16):
        got = None
        for d in range(2):
            for c in range(4):
                term = got_ref[d * 64 + block * 4 + c].astype(f32)
                got = term if got is None else got + term
        rows = DECAY * old_rows_ref[block : block + 1, :] + (1.0 - DECAY) * (got[0:1] / C)
        all_rows[block : block + 1, :] = rows
        update_sum = update_sum + got[1:2] / rows
        row_sum = row_sum + rows
        weight_sum = got[3:4]
        theirs = got_ref[(1 - lax.axis_index("dp")) * 64 + block * 4 + lax.axis_index("col")].astype(f32)
        early_ref[block : block + 1, :] = theirs[2:3]
        early_ref[16 + block : 17 + block, :] = theirs[3:4]
    row_mean = jnp.sum(row_sum, axis=1, keepdims=True) / R
    rows = all_rows[pl.ds(lax.axis_index("row"), 1), :]
    rows_ref[...] = rows
    row_scale[...] = down(lax.rsqrt(rows / row_mean))
    col_scale[...] = lax.rsqrt(cols_ref[...])
    update_mean = jnp.sum(update_sum, axis=1, keepdims=True) * row_mean / (R * C)
    weight_mean = jnp.sum(weight_sum, axis=1, keepdims=True) / (R * C)
    clip_factor = jnp.maximum(1.0, jnp.sqrt(update_mean))
    param_scale = jnp.maximum(0.001, jnp.sqrt(weight_mean))
    clip_ref[...] = clip_factor
    scale_ref[...] = param_scale
    step_size = RELATIVE * param_scale / clip_factor
    step_ref[...] = step_size
    params_copy.wait()
    weights_piece(grad, params, out_ref, row_scale[...], col_scale, step_size, start // LANES)


def weights_kernel(start, grad, params_ref, row_scale, col_scale, step_ref, out_ref, params, sem):
    (copy,) = begin((params_ref.at[:, start : start + params.shape[1]], params, sem))
    copy.wait()
    weights_piece(grad, params, out_ref, row_scale[...], col_scale, step_ref[...], start // LANES)


def params_kernel(
    grad, params_ref, row_scale, col_scale, step_ref,
    new_ref, update_ref, weights_ref, params, update, new, weights, sems, out_sems,
):
    width = grad.shape[1]
    mine = lax.axis_index("dp") * width
    pieces = steps(width)
    ins = [
        begin((params_ref.at[:, s : s + n], params.at[:, s : s + n], sems.at[i]))[0] for i, (s, n) in enumerate(pieces)
    ]
    across, step_size = row_scale[...], step_ref[...]
    outs = []
    for i, (s, n) in enumerate(pieces):
        ins[i].wait()
        for t in range(s // LANES, (s + n) // LANES):
            value = grad[:, tile(t)] * across * col_scale[t : t + 1, :]
            moved = params[:, tile(t)] - step_size * value
            update[:, tile(t)] = value
            new[:, tile(t)] = moved
            weights[:, tile(t)] = moved.astype(bf16)
        outs += begin(
            (update.at[:, s : s + n], update_ref.at[:, s : s + n], out_sems.at[3 * i]),
            (new.at[:, s : s + n], new_ref.at[:, s : s + n], out_sems.at[3 * i + 1]),
            (weights.at[:, s : s + n], weights_ref.at[:, span(mine + s, n)], out_sems.at[3 * i + 2]),
        )
    for copy in outs:
        copy.wait()


def early_kernel(width, grad_ref, ahead_ref, row_scale, scale, step_ref, _, out_ref, mine, got, out, sems, out_sem):
    count = mine.shape[1]
    first = (1 - lax.axis_index("dp")) * width
    ins = begin((grad_ref.at[0, :, span(first, count)], mine, sems.at[0]), (ahead_ref, got, sems.at[1]))
    across, step_size = row_scale[...], step_ref[...]
    for copy in ins:
        copy.wait()
    for t in range(count // LANES):
        g = mine[:, tile(t)].astype(f32) + got[:, tile(t)].astype(f32)
        update = g * across * scale[t : t + 1, :]
        out[:, tile(t)] = (got[:, tile(count // LANES + t)].astype(f32) - step_size * update).astype(bf16)
    (copy,) = begin((out, out_ref.at[:, span(first, count)], out_sem))
    copy.wait()


def place_kernel(start, width, got, _, out_ref, sem):
    first = (1 - lax.axis_index("dp")) * width + start
    (copy,) = begin((got, out_ref.at[:, span(first, got.shape[1])], sem))
    copy.wait()


HBM, VMEM = pltpu.HBM, pltpu.VMEM
dma = pltpu.SemaphoreType.DMA


def call(kernel, ins, outs, scratch, args, nbytes, aliases=None, limit=VMEM_LIMIT):
    return pl.pallas_call(
        kernel,
        in_specs=[pl.BlockSpec(memory_space=space) for space in ins],
        out_specs=[pl.BlockSpec(memory_space=space) for space, _ in outs],
        out_shape=[out for _, out in outs],
        scratch_shapes=list(scratch),
        input_output_aliases=aliases or {},
        cost_estimate=pl.CostEstimate(flops=nbytes, bytes_accessed=nbytes, transcendentals=0),
        compiler_params=pltpu.CompilerParams(vmem_limit_bytes=limit),
    )(*args)


def shards(params, grad_parts, row_moment, col_moment):
    rows, width = params.shape
    height = width // LANES
    padded = -(-height // 16) * 16
    early = EARLY * BLOCK
    count = len(steps(width))

    (outgoing,) = call(
        half_kernel, [HBM], [(HBM, shape((rows, width), bf16))],
        [VMEM((rows, width), bf16), dma((count,)), dma((count,))], (grad_parts,), 4 * rows * width,
    )
    got = lax.ppermute(outgoing, "dp", SWAP)
    ahead, weight_part = call(
        prepare_kernel, [HBM, HBM, HBM],
        [(HBM, shape((rows, 2 * early), bf16)), (VMEM, shape((1, 1), f32))],
        [VMEM((rows, width), f32), VMEM((rows, early), bf16), VMEM((rows, early), bf16), dma((count + 1,)), dma((2,))],
        (grad_parts, params, outgoing), 4 * rows * (width + early),
    )
    ahead = lax.ppermute(ahead, "dp", SWAP)

    gradient, row_part, sent = call(
        sums_kernel, [HBM, VMEM, VMEM, VMEM],
        [(VMEM, shape((rows, width), f32)), (VMEM, shape((1, rows), f32)),
         (VMEM, shape((16, padded, LANES), bf16))],
        [VMEM((rows, width), bf16), VMEM((padded, LANES), f32), dma((count,))],
        (grad_parts, got, row_moment.reshape(1, rows), weight_part), 8 * rows * width,
    )
    col_parts = lax.all_to_all(sent, "row", 0, 0)
    new_cols, cols_copy, old_rows, sent = call(
        moments_kernel, [VMEM] * 4,
        [(VMEM, shape((height, LANES), f32)), (VMEM, shape((height, LANES), f32)),
         (VMEM, shape((16, LANES), f32)), (VMEM, shape((128, 4, LANES), bf16))],
        [VMEM((height, LANES), f32)] * 2, (gradient, col_parts, row_part, col_moment.reshape(2 * height, LANES)),
        4 * rows * width,
    )
    parts = lax.all_to_all(sent, ("dp", "row", "col"), 0, 0)

    n = LATE[0] * BLOCK
    out, new_rows, clip_factor, param_scale, step_size, row_scale, col_scale, early_scale = call(
        first_weights_kernel, [VMEM, VMEM, VMEM, VMEM, HBM],
        [(VMEM, shape((rows, n), bf16)), (VMEM, shape((1, rows), f32)),
         (VMEM, shape((1, 1), f32)), (VMEM, shape((1, 1), f32)), (VMEM, shape((1, 1), f32)),
         (VMEM, shape((rows, LANES), f32)), (VMEM, shape((height, LANES), f32)), (VMEM, shape((32, LANES), f32))],
        [VMEM((rows, n), f32), VMEM((16, LANES), f32), dma],
        (parts, cols_copy, old_rows, gradient, params), 8 * rows * n,
    )
    late = [lax.ppermute(out, "dp", SWAP)]
    start = early + n
    for blocks in LATE[1:]:
        n = blocks * BLOCK
        (out,) = call(
            functools.partial(weights_kernel, start), [VMEM, HBM, VMEM, VMEM, VMEM],
            [(VMEM, shape((rows, n), bf16))], [VMEM((rows, n), f32), dma],
            (gradient, params, row_scale, col_scale, step_size), 8 * rows * n,
        )
        late.append(lax.ppermute(out, "dp", SWAP))
        start += n

    out_shape = shape((rows, 2 * width), bf16)
    new_params, update, new_weights = call(
        params_kernel, [VMEM, HBM, VMEM, VMEM, VMEM],
        [(HBM, shape((rows, width), f32)), (HBM, shape((rows, width), f32)), (HBM, out_shape)],
        [VMEM((rows, width), f32)] * 3 + [VMEM((rows, width), bf16), dma((count,)), dma((3 * count,))],
        (gradient, params, row_scale, col_scale, step_size), 18 * rows * width,
    )
    (new_weights,) = call(
        functools.partial(early_kernel, width), [HBM, HBM, VMEM, VMEM, VMEM, HBM], [(HBM, out_shape)],
        [VMEM((rows, early), bf16), VMEM((rows, 2 * early), bf16), VMEM((rows, early), bf16), dma((2,)), dma],
        (grad_parts, ahead, row_scale, early_scale, step_size, new_weights), 8 * rows * early, {5: 0},
    )
    start = early
    for blocks, values in zip(LATE, late):
        n = blocks * BLOCK
        (new_weights,) = call(
            functools.partial(place_kernel, start, width), [VMEM, HBM], [(HBM, out_shape)],
            [dma], (values, new_weights), 4 * rows * n, {1: 0},
        )
        start += n
    return (
        new_params, new_weights, new_rows.reshape(rows), new_cols.reshape(width), update,
        clip_factor.reshape(()), param_scale.reshape(()),
    )


def solution(mesh):
    in_specs = (P("row", ("col", "dp")), P("dp", "row", "col"), P("row"), P("col"))
    out_specs = (
        P("row", ("col", "dp")),
        P("row", "col"),
        P("row"),
        P(("col", "dp")),
        P("row", ("col", "dp")),
        P(),
        P(),
    )
    return jax.shard_map(shards, mesh=mesh, in_specs=in_specs, out_specs=out_specs, check_vma=False)
```

```python
import functools

import jax
import jax.numpy as jnp
from jax import lax
from jax.experimental import pallas as pl
from jax.experimental.pallas import tpu as pltpu
from jax.sharding import PartitionSpec as P

R = 2048
C = 36864
STEP = 10
DECAY = 1.0 - STEP ** (-0.8)
RELATIVE = min(0.01, STEP ** (-0.5))
LANES = 128
SWAP = [(0, 1), (1, 0)]
BLOCK = 256
WIDE = 1536
EARLY = 11
LATE = (7,)
VMEM_LIMIT = 24 << 20
f32, bf16 = jnp.float32, jnp.bfloat16
shape = jax.ShapeDtypeStruct


def down(row):
    return jnp.broadcast_to(row, (LANES, LANES)).T


def flat(acc):
    return jnp.sum(acc.T, axis=0, keepdims=True)


def split(value, count):
    parts = []
    for _ in range(count):
        parts.append(value.astype(bf16).astype(f32))
        value = value - parts[-1]
    return parts


def lanes(value):
    at = lax.broadcasted_iota(jnp.int32, (1, LANES), 1)
    row = jnp.zeros((1, LANES), f32)
    for i, part in enumerate(split(jnp.broadcast_to(value, (1, LANES)), 3)):
        row = jnp.where(at == i, part, row)
    return row


def tile(at):
    return slice(at * LANES, (at + 1) * LANES)


def span(start, count):
    return pl.ds(pl.multiple_of(start, LANES), count)


def begin(*copies):
    copies = [pltpu.make_async_copy(*copy) for copy in copies]
    for copy in copies:
        copy.start()
    return copies


def steps(width):
    return [(start, WIDE) for start in range(0, width, WIDE)]


def half_kernel(grad_ref, out_ref, sems):
    width = out_ref.shape[1]
    other = (1 - lax.axis_index("dp")) * width
    copies = [
        begin((grad_ref.at[0, :, span(other + s, n)], out_ref.at[:, s : s + n], sems.at[i]))[0]
        for i, (s, n) in enumerate(steps(width))
    ]
    for copy in copies:
        copy.wait()


def prepare_kernel(grad_ref, params_ref, _, ahead_ref, weight_ref, params, parts, values, sems, out_sems):
    width, early = params.shape[1], parts.shape[1]
    mine = lax.axis_index("dp") * width
    pieces = steps(width)
    grad = begin((grad_ref.at[0, :, span(mine, early)], parts, sems.at[len(pieces)]))[0]
    ins = [
        begin((params_ref.at[:, s : s + n], params.at[:, s : s + n], sems.at[i]))[0] for i, (s, n) in enumerate(pieces)
    ]
    acc = jnp.zeros((LANES, LANES), f32)
    for i, (s, n) in enumerate(pieces):
        ins[i].wait()
        for t in range(s // LANES, (s + n) // LANES):
            value = params[:, tile(t)]
            acc = acc + value * value
            if t < early // LANES:
                values[:, tile(t)] = value.astype(bf16)
    grad.wait()
    outs = begin(
        (parts, ahead_ref.at[:, 0:early], out_sems.at[0]), (values, ahead_ref.at[:, early : 2 * early], out_sems.at[1])
    )
    weight_ref[...] = jnp.sum(jnp.sum(acc, axis=0, keepdims=True), axis=1, keepdims=True)
    for copy in outs:
        copy.wait()


def sums_kernel(grad_parts_ref, got, old_rows_ref, weight_ref, grad, row_ref, sent_ref, mine, cols, sems):
    width = grad.shape[1]
    first = lax.axis_index("dp") * width
    pieces = steps(width)
    ins = [
        begin((grad_parts_ref.at[0, :, span(first + s, n)], mine.at[:, s : s + n], sems.at[i]))[0]
        for i, (s, n) in enumerate(pieces)
    ]
    cols[...] = jnp.zeros_like(cols)
    acc = jnp.zeros((LANES, LANES), f32)
    for i, (s, n) in enumerate(pieces):
        ins[i].wait()
        for t in range(s // LANES, (s + n) // LANES):
            g = mine[:, tile(t)].astype(f32) + got[:, tile(t)].astype(f32)
            grad[:, tile(t)] = g
            squares = g * g + 1e-30
            acc = acc + squares
            cols[t : t + 1, :] = jnp.sum(squares, axis=0, keepdims=True)
    row_ref[...] = flat(acc)
    free = width // LANES
    for i, part in enumerate(split(old_rows_ref[...], 2) + [lanes(weight_ref[...])]):
        cols[free + i : free + i + 1, :] = part
    sent = cols[...].astype(bf16)
    for peer in range(sent_ref.shape[0]):
        sent_ref[peer] = sent


def moments_kernel(
    grad, got_ref, row_ref, old_cols_ref, new_cols_ref, copy_ref, old_rows_ref, sent_ref, inv_cols, scale,
):
    height = grad.shape[1] // LANES
    totals = got_ref[0].astype(f32)
    for peer in range(1, got_ref.shape[0]):
        totals = totals + got_ref[peer].astype(f32)
    for peer in range(got_ref.shape[0]):
        rows = got_ref[peer].astype(f32)
        old_rows_ref[peer : peer + 1, :] = rows[height : height + 1] + rows[height + 1 : height + 2]
    weight = jnp.sum(totals[height + 2 : height + 3], axis=1, keepdims=True)
    old_cols = jnp.where(lax.axis_index("dp") == 0, old_cols_ref[:height], old_cols_ref[height:])
    new_cols = DECAY * old_cols + (1.0 - DECAY) * (totals[:height] / R)
    new_cols_ref[...] = new_cols
    copy_ref[...] = new_cols
    inv_cols[...] = 1.0 / new_cols
    acc = jnp.zeros((LANES, LANES), f32)
    for t in range(height):
        g = grad[:, tile(t)]
        acc = acc + g * g * inv_cols[t : t + 1, :]
    scale[...] = lax.rsqrt(new_cols)
    index = lax.axis_index("row")
    second = jnp.where(index == 15, lanes(weight), scale[pl.ds(16 + index, 1), :])
    at = lax.broadcasted_iota(jnp.int32, (4, LANES), 0)
    value = jnp.zeros((4, LANES), f32)
    for i, row in enumerate([row_ref[...], flat(acc), scale[pl.ds(index, 1), :], second]):
        value = jnp.where(at == i, jnp.broadcast_to(row, (4, LANES)), value)
    value = value.astype(bf16)
    sent_ref[...] = jnp.broadcast_to(value[None], sent_ref.shape)


def weights_piece(grad, params, out_ref, row_scale, col_scale, step_size, first):
    for t in range(params.shape[1] // LANES):
        update = grad[:, tile(first + t)] * row_scale * col_scale[first + t : first + t + 1, :]
        out_ref[:, tile(t)] = (params[:, tile(t)] - step_size * update).astype(bf16)


def first_weights_kernel(
    got_ref, cols_ref, old_rows_ref, grad, params_ref,
    out_ref, rows_ref, clip_ref, scale_ref, step_ref, row_scale, col_scale, early_ref, params, all_rows, sem,
):
    start, count = EARLY * BLOCK, params.shape[1]
    (params_copy,) = begin((params_ref.at[:, start : start + count], params, sem))
    update_sum = jnp.zeros((1, LANES), f32)
    row_sum = jnp.zeros((1, LANES), f32)
    for block in range(16):
        got = None
        for d in range(2):
            for c in range(4):
                term = got_ref[d * 64 + block * 4 + c].astype(f32)
                got = term if got is None else got + term
        rows = DECAY * old_rows_ref[block : block + 1, :] + (1.0 - DECAY) * (got[0:1] / C)
        all_rows[block : block + 1, :] = rows
        update_sum = update_sum + got[1:2] / rows
        row_sum = row_sum + rows
        weight_sum = got[3:4]
        theirs = got_ref[(1 - lax.axis_index("dp")) * 64 + block * 4 + lax.axis_index("col")].astype(f32)
        early_ref[block : block + 1, :] = theirs[2:3]
        early_ref[16 + block : 17 + block, :] = theirs[3:4]
    row_mean = jnp.sum(row_sum, axis=1, keepdims=True) / R
    rows = all_rows[pl.ds(lax.axis_index("row"), 1), :]
    rows_ref[...] = rows
    row_scale[...] = down(lax.rsqrt(rows / row_mean))
    col_scale[...] = lax.rsqrt(cols_ref[...])
    update_mean = jnp.sum(update_sum, axis=1, keepdims=True) * row_mean / (R * C)
    weight_mean = jnp.sum(weight_sum, axis=1, keepdims=True) / (R * C)
    clip_factor = jnp.maximum(1.0, jnp.sqrt(update_mean))
    param_scale = jnp.maximum(0.001, jnp.sqrt(weight_mean))
    clip_ref[...] = clip_factor
    scale_ref[...] = param_scale
    step_size = RELATIVE * param_scale / clip_factor
    step_ref[...] = step_size
    params_copy.wait()
    weights_piece(grad, params, out_ref, row_scale[...], col_scale, step_size, start // LANES)


def weights_kernel(start, grad, params_ref, row_scale, col_scale, step_ref, out_ref, params, sem):
    (copy,) = begin((params_ref.at[:, start : start + params.shape[1]], params, sem))
    copy.wait()
    weights_piece(grad, params, out_ref, row_scale[...], col_scale, step_ref[...], start // LANES)


def params_kernel(
    grad, params_ref, row_scale, col_scale, step_ref,
    new_ref, update_ref, weights_ref, params, update, new, weights, sems, out_sems,
):
    width = grad.shape[1]
    mine = lax.axis_index("dp") * width
    pieces = steps(width)
    ins = [
        begin((params_ref.at[:, s : s + n], params.at[:, s : s + n], sems.at[i]))[0] for i, (s, n) in enumerate(pieces)
    ]
    across, step_size = row_scale[...], step_ref[...]
    outs = []
    for i, (s, n) in enumerate(pieces):
        ins[i].wait()
        for t in range(s // LANES, (s + n) // LANES):
            value = grad[:, tile(t)] * across * col_scale[t : t + 1, :]
            moved = params[:, tile(t)] - step_size * value
            update[:, tile(t)] = value
            new[:, tile(t)] = moved
            weights[:, tile(t)] = moved.astype(bf16)
        outs += begin(
            (update.at[:, s : s + n], update_ref.at[:, s : s + n], out_sems.at[3 * i]),
            (new.at[:, s : s + n], new_ref.at[:, s : s + n], out_sems.at[3 * i + 1]),
            (weights.at[:, s : s + n], weights_ref.at[:, span(mine + s, n)], out_sems.at[3 * i + 2]),
        )
    for copy in outs:
        copy.wait()


def early_kernel(width, grad_ref, ahead_ref, row_scale, scale, step_ref, _, out_ref, mine, got, out, sems, out_sem):
    count = mine.shape[1]
    first = (1 - lax.axis_index("dp")) * width
    ins = begin((grad_ref.at[0, :, span(first, count)], mine, sems.at[0]), (ahead_ref, got, sems.at[1]))
    across, step_size = row_scale[...], step_ref[...]
    for copy in ins:
        copy.wait()
    for t in range(count // LANES):
        g = mine[:, tile(t)].astype(f32) + got[:, tile(t)].astype(f32)
        update = g * across * scale[t : t + 1, :]
        out[:, tile(t)] = (got[:, tile(count // LANES + t)].astype(f32) - step_size * update).astype(bf16)
    (copy,) = begin((out, out_ref.at[:, span(first, count)], out_sem))
    copy.wait()


def place_kernel(start, width, got, _, out_ref, sem):
    first = (1 - lax.axis_index("dp")) * width + start
    (copy,) = begin((got, out_ref.at[:, span(first, got.shape[1])], sem))
    copy.wait()


HBM, VMEM = pltpu.HBM, pltpu.VMEM
dma = pltpu.SemaphoreType.DMA


def call(kernel, ins, outs, scratch, args, nbytes, aliases=None, limit=VMEM_LIMIT):
    return pl.pallas_call(
        kernel,
        in_specs=[pl.BlockSpec(memory_space=space) for space in ins],
        out_specs=[pl.BlockSpec(memory_space=space) for space, _ in outs],
        out_shape=[out for _, out in outs],
        scratch_shapes=list(scratch),
        input_output_aliases=aliases or {},
        cost_estimate=pl.CostEstimate(flops=nbytes, bytes_accessed=nbytes, transcendentals=0),
        compiler_params=pltpu.CompilerParams(vmem_limit_bytes=limit),
    )(*args)


def shards(params, grad_parts, row_moment, col_moment):
    rows, width = params.shape
    height = width // LANES
    padded = -(-height // 16) * 16
    early = EARLY * BLOCK
    count = len(steps(width))

    (outgoing,) = call(
        half_kernel, [HBM], [(VMEM, shape((rows, width), bf16))], [dma((count,))],
        (pltpu.with_memory_space_constraint(grad_parts, HBM),), 4 * rows * width,
    )
    got = lax.ppermute(outgoing, "dp", SWAP)
    ahead, weight_part = call(
        prepare_kernel, [HBM, HBM, HBM],
        [(HBM, shape((rows, 2 * early), bf16)), (VMEM, shape((1, 1), f32))],
        [VMEM((rows, width), f32), VMEM((rows, early), bf16), VMEM((rows, early), bf16), dma((count + 1,)), dma((2,))],
        (grad_parts, params, outgoing), 4 * rows * (width + early),
    )
    ahead = lax.ppermute(ahead, "dp", SWAP)

    gradient, row_part, sent = call(
        sums_kernel, [HBM, VMEM, VMEM, VMEM],
        [(VMEM, shape((rows, width), f32)), (VMEM, shape((1, rows), f32)),
         (VMEM, shape((16, padded, LANES), bf16))],
        [VMEM((rows, width), bf16), VMEM((padded, LANES), f32), dma((count,))],
        (grad_parts, got, row_moment.reshape(1, rows), weight_part), 8 * rows * width,
    )
    col_parts = lax.all_to_all(sent, "row", 0, 0)
    new_cols, cols_copy, old_rows, sent = call(
        moments_kernel, [VMEM] * 4,
        [(VMEM, shape((height, LANES), f32)), (VMEM, shape((height, LANES), f32)),
         (VMEM, shape((16, LANES), f32)), (VMEM, shape((128, 4, LANES), bf16))],
        [VMEM((height, LANES), f32)] * 2, (gradient, col_parts, row_part, col_moment.reshape(2 * height, LANES)),
        4 * rows * width,
    )
    parts = lax.all_to_all(sent, ("dp", "row", "col"), 0, 0)

    n = LATE[0] * BLOCK
    out, new_rows, clip_factor, param_scale, step_size, row_scale, col_scale, early_scale = call(
        first_weights_kernel, [VMEM, VMEM, VMEM, VMEM, HBM],
        [(VMEM, shape((rows, n), bf16)), (VMEM, shape((1, rows), f32)),
         (VMEM, shape((1, 1), f32)), (VMEM, shape((1, 1), f32)), (VMEM, shape((1, 1), f32)),
         (VMEM, shape((rows, LANES), f32)), (VMEM, shape((height, LANES), f32)), (VMEM, shape((32, LANES), f32))],
        [VMEM((rows, n), f32), VMEM((16, LANES), f32), dma],
        (parts, cols_copy, old_rows, gradient, params), 8 * rows * n,
    )
    late = [lax.ppermute(out, "dp", SWAP)]
    start = early + n
    for blocks in LATE[1:]:
        n = blocks * BLOCK
        (out,) = call(
            functools.partial(weights_kernel, start), [VMEM, HBM, VMEM, VMEM, VMEM],
            [(VMEM, shape((rows, n), bf16))], [VMEM((rows, n), f32), dma],
            (gradient, params, row_scale, col_scale, step_size), 8 * rows * n,
        )
        late.append(lax.ppermute(out, "dp", SWAP))
        start += n

    out_shape = shape((rows, 2 * width), bf16)
    new_params, update, new_weights = call(
        params_kernel, [VMEM, HBM, VMEM, VMEM, VMEM],
        [(HBM, shape((rows, width), f32)), (HBM, shape((rows, width), f32)), (HBM, out_shape)],
        [VMEM((rows, width), f32)] * 3 + [VMEM((rows, width), bf16), dma((count,)), dma((3 * count,))],
        (gradient, params, row_scale, col_scale, step_size), 18 * rows * width,
    )
    (new_weights,) = call(
        functools.partial(early_kernel, width), [HBM, HBM, VMEM, VMEM, VMEM, HBM], [(HBM, out_shape)],
        [VMEM((rows, early), bf16), VMEM((rows, 2 * early), bf16), VMEM((rows, early), bf16), dma((2,)), dma],
        (grad_parts, ahead, row_scale, early_scale, step_size, new_weights), 8 * rows * early, {5: 0},
    )
    start = early
    for blocks, values in zip(LATE, late):
        n = blocks * BLOCK
        (new_weights,) = call(
            functools.partial(place_kernel, start, width), [VMEM, HBM], [(HBM, out_shape)],
            [dma], (values, new_weights), 4 * rows * n, {1: 0},
        )
        start += n
    return (
        new_params, new_weights, new_rows.reshape(rows), new_cols.reshape(width), update,
        clip_factor.reshape(()), param_scale.reshape(()),
    )


def solution(mesh):
    in_specs = (P("row", ("col", "dp")), P("dp", "row", "col"), P("row"), P("col"))
    out_specs = (
        P("row", ("col", "dp")),
        P("row", "col"),
        P("row"),
        P(("col", "dp")),
        P("row", ("col", "dp")),
        P(),
        P(),
    )
    return jax.shard_map(shards, mesh=mesh, in_specs=in_specs, out_specs=out_specs, check_vma=False)
```

```python
import functools

import jax
import jax.numpy as jnp
from jax import lax
from jax.experimental import pallas as pl
from jax.experimental.pallas import tpu as pltpu
from jax.sharding import PartitionSpec as P

R = 2048
C = 36864
STEP = 10
DECAY = 1.0 - STEP ** (-0.8)
RELATIVE = min(0.01, STEP ** (-0.5))
LANES = 128
SWAP = [(0, 1), (1, 0)]
BLOCK = 256
WIDE = 1536
EARLY = 11
LATE = (5, 2)
VMEM_LIMIT = 24 << 20
f32, bf16 = jnp.float32, jnp.bfloat16
shape = jax.ShapeDtypeStruct


def down(row):
    return jnp.broadcast_to(row, (LANES, LANES)).T


def flat(acc):
    return jnp.sum(acc.T, axis=0, keepdims=True)


def split(value, count):
    parts = []
    for _ in range(count):
        parts.append(value.astype(bf16).astype(f32))
        value = value - parts[-1]
    return parts


def lanes(value):
    at = lax.broadcasted_iota(jnp.int32, (1, LANES), 1)
    row = jnp.zeros((1, LANES), f32)
    for i, part in enumerate(split(jnp.broadcast_to(value, (1, LANES)), 3)):
        row = jnp.where(at == i, part, row)
    return row


def tile(at):
    return slice(at * LANES, (at + 1) * LANES)


def span(start, count):
    return pl.ds(pl.multiple_of(start, LANES), count)


def begin(*copies):
    copies = [pltpu.make_async_copy(*copy) for copy in copies]
    for copy in copies:
        copy.start()
    return copies


def steps(width):
    return [(start, WIDE) for start in range(0, width, WIDE)]


def half_kernel(grad_ref, out_ref, sems):
    width = out_ref.shape[1]
    other = (1 - lax.axis_index("dp")) * width
    copies = [
        begin((grad_ref.at[0, :, span(other + s, n)], out_ref.at[:, s : s + n], sems.at[i]))[0]
        for i, (s, n) in enumerate(steps(width))
    ]
    for copy in copies:
        copy.wait()


def prepare_kernel(grad_ref, params_ref, _, ahead_ref, weight_ref, params, parts, values, sems, out_sems):
    width, early = params.shape[1], parts.shape[1]
    mine = lax.axis_index("dp") * width
    pieces = steps(width)
    grad = begin((grad_ref.at[0, :, span(mine, early)], parts, sems.at[len(pieces)]))[0]
    ins = [
        begin((params_ref.at[:, s : s + n], params.at[:, s : s + n], sems.at[i]))[0] for i, (s, n) in enumerate(pieces)
    ]
    acc = jnp.zeros((LANES, LANES), f32)
    for i, (s, n) in enumerate(pieces):
        ins[i].wait()
        for t in range(s // LANES, (s + n) // LANES):
            value = params[:, tile(t)]
            acc = acc + value * value
            if t < early // LANES:
                values[:, tile(t)] = value.astype(bf16)
    grad.wait()
    outs = begin(
        (parts, ahead_ref.at[:, 0:early], out_sems.at[0]), (values, ahead_ref.at[:, early : 2 * early], out_sems.at[1])
    )
    weight_ref[...] = jnp.sum(jnp.sum(acc, axis=0, keepdims=True), axis=1, keepdims=True)
    for copy in outs:
        copy.wait()


def sums_kernel(grad_parts_ref, got, old_rows_ref, weight_ref, grad, row_ref, sent_ref, mine, cols, sems):
    width = grad.shape[1]
    first = lax.axis_index("dp") * width
    pieces = steps(width)
    ins = [
        begin((grad_parts_ref.at[0, :, span(first + s, n)], mine.at[:, s : s + n], sems.at[i]))[0]
        for i, (s, n) in enumerate(pieces)
    ]
    cols[...] = jnp.zeros_like(cols)
    acc = jnp.zeros((LANES, LANES), f32)
    for i, (s, n) in enumerate(pieces):
        ins[i].wait()
        for t in range(s // LANES, (s + n) // LANES):
            g = mine[:, tile(t)].astype(f32) + got[:, tile(t)].astype(f32)
            grad[:, tile(t)] = g
            squares = g * g + 1e-30
            acc = acc + squares
            cols[t : t + 1, :] = jnp.sum(squares, axis=0, keepdims=True)
    row_ref[...] = flat(acc)
    free = width // LANES
    for i, part in enumerate(split(old_rows_ref[...], 2) + [lanes(weight_ref[...])]):
        cols[free + i : free + i + 1, :] = part
    sent = cols[...].astype(bf16)
    for peer in range(sent_ref.shape[0]):
        sent_ref[peer] = sent


def moments_kernel(
    grad, got_ref, row_ref, old_cols_ref, new_cols_ref, copy_ref, old_rows_ref, sent_ref, inv_cols, scale,
):
    height = grad.shape[1] // LANES
    totals = got_ref[0].astype(f32)
    for peer in range(1, got_ref.shape[0]):
        totals = totals + got_ref[peer].astype(f32)
    for peer in range(got_ref.shape[0]):
        rows = got_ref[peer].astype(f32)
        old_rows_ref[peer : peer + 1, :] = rows[height : height + 1] + rows[height + 1 : height + 2]
    weight = jnp.sum(totals[height + 2 : height + 3], axis=1, keepdims=True)
    old_cols = jnp.where(lax.axis_index("dp") == 0, old_cols_ref[:height], old_cols_ref[height:])
    new_cols = DECAY * old_cols + (1.0 - DECAY) * (totals[:height] / R)
    new_cols_ref[...] = new_cols
    copy_ref[...] = new_cols
    inv_cols[...] = 1.0 / new_cols
    acc = jnp.zeros((LANES, LANES), f32)
    for t in range(height):
        g = grad[:, tile(t)]
        acc = acc + g * g * inv_cols[t : t + 1, :]
    scale[...] = lax.rsqrt(new_cols)
    index = lax.axis_index("row")
    second = jnp.where(index == 15, lanes(weight), scale[pl.ds(16 + index, 1), :])
    at = lax.broadcasted_iota(jnp.int32, (4, LANES), 0)
    value = jnp.zeros((4, LANES), f32)
    for i, row in enumerate([row_ref[...], flat(acc), scale[pl.ds(index, 1), :], second]):
        value = jnp.where(at == i, jnp.broadcast_to(row, (4, LANES)), value)
    value = value.astype(bf16)
    sent_ref[...] = jnp.broadcast_to(value[None], sent_ref.shape)


def weights_piece(grad, params, out_ref, row_scale, col_scale, step_size, first):
    for t in range(params.shape[1] // LANES):
        update = grad[:, tile(first + t)] * row_scale * col_scale[first + t : first + t + 1, :]
        out_ref[:, tile(t)] = (params[:, tile(t)] - step_size * update).astype(bf16)


def first_weights_kernel(
    got_ref, cols_ref, old_rows_ref, grad, params_ref,
    out_ref, rows_ref, clip_ref, scale_ref, step_ref, row_scale, col_scale, early_ref, params, all_rows, sem,
):
    start, count = EARLY * BLOCK, params.shape[1]
    (params_copy,) = begin((params_ref.at[:, start : start + count], params, sem))
    update_sum = jnp.zeros((1, LANES), f32)
    row_sum = jnp.zeros((1, LANES), f32)
    for block in range(16):
        got = None
        for d in range(2):
            for c in range(4):
                term = got_ref[d * 64 + block * 4 + c].astype(f32)
                got = term if got is None else got + term
        rows = DECAY * old_rows_ref[block : block + 1, :] + (1.0 - DECAY) * (got[0:1] / C)
        all_rows[block : block + 1, :] = rows
        update_sum = update_sum + got[1:2] / rows
        row_sum = row_sum + rows
        weight_sum = got[3:4]
        theirs = got_ref[(1 - lax.axis_index("dp")) * 64 + block * 4 + lax.axis_index("col")].astype(f32)
        early_ref[block : block + 1, :] = theirs[2:3]
        early_ref[16 + block : 17 + block, :] = theirs[3:4]
    row_mean = jnp.sum(row_sum, axis=1, keepdims=True) / R
    rows = all_rows[pl.ds(lax.axis_index("row"), 1), :]
    rows_ref[...] = rows
    row_scale[...] = down(lax.rsqrt(rows / row_mean))
    col_scale[...] = lax.rsqrt(cols_ref[...])
    update_mean = jnp.sum(update_sum, axis=1, keepdims=True) * row_mean / (R * C)
    weight_mean = jnp.sum(weight_sum, axis=1, keepdims=True) / (R * C)
    clip_factor = jnp.maximum(1.0, jnp.sqrt(update_mean))
    param_scale = jnp.maximum(0.001, jnp.sqrt(weight_mean))
    clip_ref[...] = clip_factor
    scale_ref[...] = param_scale
    step_size = RELATIVE * param_scale / clip_factor
    step_ref[...] = step_size
    params_copy.wait()
    weights_piece(grad, params, out_ref, row_scale[...], col_scale, step_size, start // LANES)


def weights_kernel(start, grad, params_ref, row_scale, col_scale, step_ref, out_ref, params, sem):
    (copy,) = begin((params_ref.at[:, start : start + params.shape[1]], params, sem))
    copy.wait()
    weights_piece(grad, params, out_ref, row_scale[...], col_scale, step_ref[...], start // LANES)


def params_kernel(
    grad, params_ref, row_scale, col_scale, step_ref,
    new_ref, update_ref, weights_ref, params, update, new, weights, sems, out_sems,
):
    width = grad.shape[1]
    mine = lax.axis_index("dp") * width
    pieces = steps(width)
    ins = [
        begin((params_ref.at[:, s : s + n], params.at[:, s : s + n], sems.at[i]))[0] for i, (s, n) in enumerate(pieces)
    ]
    across, step_size = row_scale[...], step_ref[...]
    outs = []
    for i, (s, n) in enumerate(pieces):
        ins[i].wait()
        for t in range(s // LANES, (s + n) // LANES):
            value = grad[:, tile(t)] * across * col_scale[t : t + 1, :]
            moved = params[:, tile(t)] - step_size * value
            update[:, tile(t)] = value
            new[:, tile(t)] = moved
            weights[:, tile(t)] = moved.astype(bf16)
        outs += begin(
            (update.at[:, s : s + n], update_ref.at[:, s : s + n], out_sems.at[3 * i]),
            (new.at[:, s : s + n], new_ref.at[:, s : s + n], out_sems.at[3 * i + 1]),
            (weights.at[:, s : s + n], weights_ref.at[:, span(mine + s, n)], out_sems.at[3 * i + 2]),
        )
    for copy in outs:
        copy.wait()


def early_kernel(width, grad_ref, ahead_ref, row_scale, scale, step_ref, _, out_ref, mine, got, out, sems, out_sem):
    count = mine.shape[1]
    first = (1 - lax.axis_index("dp")) * width
    ins = begin((grad_ref.at[0, :, span(first, count)], mine, sems.at[0]), (ahead_ref, got, sems.at[1]))
    across, step_size = row_scale[...], step_ref[...]
    for copy in ins:
        copy.wait()
    for t in range(count // LANES):
        g = mine[:, tile(t)].astype(f32) + got[:, tile(t)].astype(f32)
        update = g * across * scale[t : t + 1, :]
        out[:, tile(t)] = (got[:, tile(count // LANES + t)].astype(f32) - step_size * update).astype(bf16)
    (copy,) = begin((out, out_ref.at[:, span(first, count)], out_sem))
    copy.wait()


def place_kernel(start, width, got, _, out_ref, sem):
    first = (1 - lax.axis_index("dp")) * width + start
    (copy,) = begin((got, out_ref.at[:, span(first, got.shape[1])], sem))
    copy.wait()


HBM, VMEM = pltpu.HBM, pltpu.VMEM
dma = pltpu.SemaphoreType.DMA


def call(kernel, ins, outs, scratch, args, nbytes, aliases=None, limit=VMEM_LIMIT):
    return pl.pallas_call(
        kernel,
        in_specs=[pl.BlockSpec(memory_space=space) for space in ins],
        out_specs=[pl.BlockSpec(memory_space=space) for space, _ in outs],
        out_shape=[out for _, out in outs],
        scratch_shapes=list(scratch),
        input_output_aliases=aliases or {},
        cost_estimate=pl.CostEstimate(flops=nbytes, bytes_accessed=nbytes, transcendentals=0),
        compiler_params=pltpu.CompilerParams(vmem_limit_bytes=limit),
    )(*args)


def shards(params, grad_parts, row_moment, col_moment):
    rows, width = params.shape
    height = width // LANES
    padded = -(-height // 16) * 16
    early = EARLY * BLOCK
    count = len(steps(width))

    (outgoing,) = call(
        half_kernel, [HBM], [(VMEM, shape((rows, width), bf16))], [dma((count,))],
        (pltpu.with_memory_space_constraint(grad_parts, HBM),), 4 * rows * width,
    )
    got = lax.ppermute(outgoing, "dp", SWAP)
    ahead, weight_part = call(
        prepare_kernel, [HBM, HBM, HBM],
        [(HBM, shape((rows, 2 * early), bf16)), (VMEM, shape((1, 1), f32))],
        [VMEM((rows, width), f32), VMEM((rows, early), bf16), VMEM((rows, early), bf16), dma((count + 1,)), dma((2,))],
        (grad_parts, params, outgoing), 4 * rows * (width + early),
    )
    ahead = lax.ppermute(ahead, "dp", SWAP)

    gradient, row_part, sent = call(
        sums_kernel, [HBM, VMEM, VMEM, VMEM],
        [(VMEM, shape((rows, width), f32)), (VMEM, shape((1, rows), f32)),
         (VMEM, shape((16, padded, LANES), bf16))],
        [VMEM((rows, width), bf16), VMEM((padded, LANES), f32), dma((count,))],
        (grad_parts, got, row_moment.reshape(1, rows), weight_part), 8 * rows * width,
    )
    col_parts = lax.all_to_all(sent, "row", 0, 0)
    new_cols, cols_copy, old_rows, sent = call(
        moments_kernel, [VMEM] * 4,
        [(VMEM, shape((height, LANES), f32)), (VMEM, shape((height, LANES), f32)),
         (VMEM, shape((16, LANES), f32)), (VMEM, shape((128, 4, LANES), bf16))],
        [VMEM((height, LANES), f32)] * 2, (gradient, col_parts, row_part, col_moment.reshape(2 * height, LANES)),
        4 * rows * width,
    )
    parts = lax.all_to_all(sent, ("dp", "row", "col"), 0, 0)

    n = LATE[0] * BLOCK
    out, new_rows, clip_factor, param_scale, step_size, row_scale, col_scale, early_scale = call(
        first_weights_kernel, [VMEM, VMEM, VMEM, VMEM, HBM],
        [(VMEM, shape((rows, n), bf16)), (VMEM, shape((1, rows), f32)),
         (VMEM, shape((1, 1), f32)), (VMEM, shape((1, 1), f32)), (VMEM, shape((1, 1), f32)),
         (VMEM, shape((rows, LANES), f32)), (VMEM, shape((height, LANES), f32)), (VMEM, shape((32, LANES), f32))],
        [VMEM((rows, n), f32), VMEM((16, LANES), f32), dma],
        (parts, cols_copy, old_rows, gradient, params), 8 * rows * n,
    )
    late = [lax.ppermute(out, "dp", SWAP)]
    start = early + n
    for blocks in LATE[1:]:
        n = blocks * BLOCK
        (out,) = call(
            functools.partial(weights_kernel, start), [VMEM, HBM, VMEM, VMEM, VMEM],
            [(VMEM, shape((rows, n), bf16))], [VMEM((rows, n), f32), dma],
            (gradient, params, row_scale, col_scale, step_size), 8 * rows * n,
        )
        late.append(lax.ppermute(out, "dp", SWAP))
        start += n

    out_shape = shape((rows, 2 * width), bf16)
    new_params, update, new_weights = call(
        params_kernel, [VMEM, HBM, VMEM, VMEM, VMEM],
        [(HBM, shape((rows, width), f32)), (HBM, shape((rows, width), f32)), (HBM, out_shape)],
        [VMEM((rows, width), f32)] * 3 + [VMEM((rows, width), bf16), dma((count,)), dma((3 * count,))],
        (gradient, params, row_scale, col_scale, step_size), 18 * rows * width,
    )
    (new_weights,) = call(
        functools.partial(early_kernel, width), [HBM, HBM, VMEM, VMEM, VMEM, HBM], [(HBM, out_shape)],
        [VMEM((rows, early), bf16), VMEM((rows, 2 * early), bf16), VMEM((rows, early), bf16), dma((2,)), dma],
        (grad_parts, ahead, row_scale, early_scale, step_size, new_weights), 8 * rows * early, {5: 0},
    )
    start = early
    for blocks, values in zip(LATE, late):
        n = blocks * BLOCK
        (new_weights,) = call(
            functools.partial(place_kernel, start, width), [VMEM, HBM], [(HBM, out_shape)],
            [dma], (values, new_weights), 4 * rows * n, {1: 0},
        )
        start += n
    return (
        new_params, new_weights, new_rows.reshape(rows), new_cols.reshape(width), update,
        clip_factor.reshape(()), param_scale.reshape(()),
    )


def solution(mesh):
    in_specs = (P("row", ("col", "dp")), P("dp", "row", "col"), P("row"), P("col"))
    out_specs = (
        P("row", ("col", "dp")),
        P("row", "col"),
        P("row"),
        P(("col", "dp")),
        P("row", ("col", "dp")),
        P(),
        P(),
    )
    return jax.shard_map(shards, mesh=mesh, in_specs=in_specs, out_specs=out_specs, check_vma=False)
```

```python
import functools

import jax
import jax.numpy as jnp
from jax import lax
from jax.experimental import pallas as pl
from jax.experimental.pallas import tpu as pltpu
from jax.sharding import PartitionSpec as P

R = 2048
C = 36864
STEP = 10
DECAY = 1.0 - STEP ** (-0.8)
RELATIVE = min(0.01, STEP ** (-0.5))
LANES = 128
SWAP = [(0, 1), (1, 0)]
BLOCK = 256
WIDE = 1536
EARLY = 11
LATE = (7,)
VMEM_LIMIT = 24 << 20
f32, bf16 = jnp.float32, jnp.bfloat16
shape = jax.ShapeDtypeStruct


def down(row):
    return jnp.broadcast_to(row, (LANES, LANES)).T


def flat(acc):
    return jnp.sum(acc.T, axis=0, keepdims=True)


def split(value, count):
    parts = []
    for _ in range(count):
        parts.append(value.astype(bf16).astype(f32))
        value = value - parts[-1]
    return parts


def lanes(value):
    at = lax.broadcasted_iota(jnp.int32, (1, LANES), 1)
    row = jnp.zeros((1, LANES), f32)
    for i, part in enumerate(split(jnp.broadcast_to(value, (1, LANES)), 3)):
        row = jnp.where(at == i, part, row)
    return row


def tile(at):
    return slice(at * LANES, (at + 1) * LANES)


def span(start, count):
    return pl.ds(pl.multiple_of(start, LANES), count)


def begin(*copies):
    copies = [pltpu.make_async_copy(*copy) for copy in copies]
    for copy in copies:
        copy.start()
    return copies


def steps(width):
    return [(start, WIDE) for start in range(0, width, WIDE)]


def half_kernel(grad_ref, out_ref, sems):
    width = out_ref.shape[1]
    other = (1 - lax.axis_index("dp")) * width
    copies = [
        begin((grad_ref.at[0, :, span(other + s, n)], out_ref.at[:, s : s + n], sems.at[i]))[0]
        for i, (s, n) in enumerate(steps(width))
    ]
    for copy in copies:
        copy.wait()


def prepare_kernel(grad_ref, params_ref, _, ahead_ref, weight_ref, params, parts, values, sems, out_sems):
    width, early = params.shape[1], parts.shape[1]
    mine = lax.axis_index("dp") * width
    pieces = steps(width)
    grad = begin((grad_ref.at[0, :, span(mine, early)], parts, sems.at[len(pieces)]))[0]
    ins = [
        begin((params_ref.at[:, s : s + n], params.at[:, s : s + n], sems.at[i]))[0] for i, (s, n) in enumerate(pieces)
    ]
    acc = jnp.zeros((LANES, LANES), f32)
    for i, (s, n) in enumerate(pieces):
        ins[i].wait()
        for t in range(s // LANES, (s + n) // LANES):
            value = params[:, tile(t)]
            acc = acc + value * value
            if t < early // LANES:
                values[:, tile(t)] = value.astype(bf16)
    grad.wait()
    outs = begin(
        (parts, ahead_ref.at[:, 0:early], out_sems.at[0]), (values, ahead_ref.at[:, early : 2 * early], out_sems.at[1])
    )
    weight_ref[...] = jnp.sum(jnp.sum(acc, axis=0, keepdims=True), axis=1, keepdims=True)
    for copy in outs:
        copy.wait()


def sums_kernel(grad_parts_ref, got, old_rows_ref, weight_ref, grad, row_ref, sent_ref, mine, cols, sems):
    width = grad.shape[1]
    first = lax.axis_index("dp") * width
    pieces = steps(width)
    ins = [
        begin((grad_parts_ref.at[0, :, span(first + s, n)], mine.at[:, s : s + n], sems.at[i]))[0]
        for i, (s, n) in enumerate(pieces)
    ]
    cols[...] = jnp.zeros_like(cols)
    acc = jnp.zeros((LANES, LANES), f32)
    for i, (s, n) in enumerate(pieces):
        ins[i].wait()
        for t in range(s // LANES, (s + n) // LANES):
            g = mine[:, tile(t)].astype(f32) + got[:, tile(t)].astype(f32)
            grad[:, tile(t)] = g
            squares = g * g + 1e-30
            acc = acc + squares
            cols[t : t + 1, :] = jnp.sum(squares, axis=0, keepdims=True)
    row_ref[...] = flat(acc)
    free = width // LANES
    for i, part in enumerate(split(old_rows_ref[...], 2) + [lanes(weight_ref[...])]):
        cols[free + i : free + i + 1, :] = part
    sent = cols[...].astype(bf16)
    for peer in range(sent_ref.shape[0]):
        sent_ref[peer] = sent


def moments_kernel(
    grad, got_ref, row_ref, old_cols_ref, new_cols_ref, copy_ref, old_rows_ref, sent_ref, inv_cols, scale,
):
    height = grad.shape[1] // LANES
    totals = got_ref[0].astype(f32)
    for peer in range(1, got_ref.shape[0]):
        totals = totals + got_ref[peer].astype(f32)
    for peer in range(got_ref.shape[0]):
        rows = got_ref[peer].astype(f32)
        old_rows_ref[peer : peer + 1, :] = rows[height : height + 1] + rows[height + 1 : height + 2]
    weight = jnp.sum(totals[height + 2 : height + 3], axis=1, keepdims=True)
    old_cols = jnp.where(lax.axis_index("dp") == 0, old_cols_ref[:height], old_cols_ref[height:])
    new_cols = DECAY * old_cols + (1.0 - DECAY) * (totals[:height] / R)
    new_cols_ref[...] = new_cols
    copy_ref[...] = new_cols
    inv_cols[...] = 1.0 / new_cols
    acc = jnp.zeros((LANES, LANES), f32)
    for t in range(height):
        g = grad[:, tile(t)]
        acc = acc + g * g * inv_cols[t : t + 1, :]
    scale[...] = lax.rsqrt(new_cols)
    index = lax.axis_index("row")
    second = jnp.where(index == 15, lanes(weight), scale[pl.ds(16 + index, 1), :])
    at = lax.broadcasted_iota(jnp.int32, (4, LANES), 0)
    value = jnp.zeros((4, LANES), f32)
    for i, row in enumerate([row_ref[...], flat(acc), scale[pl.ds(index, 1), :], second]):
        value = jnp.where(at == i, jnp.broadcast_to(row, (4, LANES)), value)
    value = value.astype(bf16)
    sent_ref[...] = jnp.broadcast_to(value[None], sent_ref.shape)


def weights_piece(grad, params, out_ref, row_scale, col_scale, step_size, first):
    for t in range(params.shape[1] // LANES):
        update = grad[:, tile(first + t)] * row_scale * col_scale[first + t : first + t + 1, :]
        out_ref[:, tile(t)] = (params[:, tile(t)] - step_size * update).astype(bf16)


def first_weights_kernel(
    got_ref, cols_ref, old_rows_ref, grad, params_ref,
    out_ref, rows_ref, clip_ref, scale_ref, step_ref, row_scale, col_scale, early_ref, params, all_rows, sem,
):
    start, count = EARLY * BLOCK, params.shape[1]
    (params_copy,) = begin((params_ref.at[:, start : start + count], params, sem))
    update_sum = jnp.zeros((1, LANES), f32)
    row_sum = jnp.zeros((1, LANES), f32)
    for block in range(16):
        got = None
        for d in range(2):
            for c in range(4):
                term = got_ref[d * 64 + block * 4 + c].astype(f32)
                got = term if got is None else got + term
        rows = DECAY * old_rows_ref[block : block + 1, :] + (1.0 - DECAY) * (got[0:1] / C)
        all_rows[block : block + 1, :] = rows
        update_sum = update_sum + got[1:2] / rows
        row_sum = row_sum + rows
        weight_sum = got[3:4]
        theirs = got_ref[(1 - lax.axis_index("dp")) * 64 + block * 4 + lax.axis_index("col")].astype(f32)
        early_ref[block : block + 1, :] = theirs[2:3]
        early_ref[16 + block : 17 + block, :] = theirs[3:4]
    row_mean = jnp.sum(row_sum, axis=1, keepdims=True) / R
    rows = all_rows[pl.ds(lax.axis_index("row"), 1), :]
    rows_ref[...] = rows
    row_scale[...] = down(lax.rsqrt(rows / row_mean))
    col_scale[...] = lax.rsqrt(cols_ref[...])
    update_mean = jnp.sum(update_sum, axis=1, keepdims=True) * row_mean / (R * C)
    weight_mean = jnp.sum(weight_sum, axis=1, keepdims=True) / (R * C)
    clip_factor = jnp.maximum(1.0, jnp.sqrt(update_mean))
    param_scale = jnp.maximum(0.001, jnp.sqrt(weight_mean))
    clip_ref[...] = clip_factor
    scale_ref[...] = param_scale
    step_size = RELATIVE * param_scale / clip_factor
    step_ref[...] = step_size
    params_copy.wait()
    weights_piece(grad, params, out_ref, row_scale[...], col_scale, step_size, start // LANES)


def weights_kernel(start, grad, params_ref, row_scale, col_scale, step_ref, out_ref, params, sem):
    (copy,) = begin((params_ref.at[:, start : start + params.shape[1]], params, sem))
    copy.wait()
    weights_piece(grad, params, out_ref, row_scale[...], col_scale, step_ref[...], start // LANES)


def params_kernel(
    grad, params_ref, row_scale, col_scale, step_ref,
    new_ref, update_ref, weights_ref, params, update, new, weights, sems, out_sems,
):
    width = grad.shape[1]
    mine = lax.axis_index("dp") * width
    pieces = steps(width)
    ins = [
        begin((params_ref.at[:, s : s + n], params.at[:, s : s + n], sems.at[i]))[0] for i, (s, n) in enumerate(pieces)
    ]
    across, step_size = row_scale[...], step_ref[...]
    outs = []
    for i, (s, n) in enumerate(pieces):
        ins[i].wait()
        for t in range(s // LANES, (s + n) // LANES):
            value = grad[:, tile(t)] * across * col_scale[t : t + 1, :]
            moved = params[:, tile(t)] - step_size * value
            update[:, tile(t)] = value
            new[:, tile(t)] = moved
            weights[:, tile(t)] = moved.astype(bf16)
        outs += begin(
            (update.at[:, s : s + n], update_ref.at[:, s : s + n], out_sems.at[3 * i]),
            (new.at[:, s : s + n], new_ref.at[:, s : s + n], out_sems.at[3 * i + 1]),
            (weights.at[:, s : s + n], weights_ref.at[:, span(mine + s, n)], out_sems.at[3 * i + 2]),
        )
    for copy in outs:
        copy.wait()


def early_kernel(width, grad_ref, ahead_ref, row_scale, scale, step_ref, _, out_ref, mine, got, out, sems, out_sem):
    count = mine.shape[1]
    first = (1 - lax.axis_index("dp")) * width
    ins = begin((grad_ref.at[0, :, span(first, count)], mine, sems.at[0]), (ahead_ref, got, sems.at[1]))
    across, step_size = row_scale[...], step_ref[...]
    for copy in ins:
        copy.wait()
    for t in range(count // LANES):
        g = mine[:, tile(t)].astype(f32) + got[:, tile(t)].astype(f32)
        update = g * across * scale[t : t + 1, :]
        out[:, tile(t)] = (got[:, tile(count // LANES + t)].astype(f32) - step_size * update).astype(bf16)
    (copy,) = begin((out, out_ref.at[:, span(first, count)], out_sem))
    copy.wait()


def place_kernel(start, width, got, _, out_ref, sem):
    first = (1 - lax.axis_index("dp")) * width + start
    (copy,) = begin((got, out_ref.at[:, span(first, got.shape[1])], sem))
    copy.wait()


HBM, VMEM = pltpu.HBM, pltpu.VMEM
dma = pltpu.SemaphoreType.DMA


def call(kernel, ins, outs, scratch, args, nbytes, aliases=None, limit=VMEM_LIMIT):
    return pl.pallas_call(
        kernel,
        in_specs=[pl.BlockSpec(memory_space=space) for space in ins],
        out_specs=[pl.BlockSpec(memory_space=space) for space, _ in outs],
        out_shape=[out for _, out in outs],
        scratch_shapes=list(scratch),
        input_output_aliases=aliases or {},
        cost_estimate=pl.CostEstimate(flops=nbytes, bytes_accessed=nbytes, transcendentals=0),
        compiler_params=pltpu.CompilerParams(vmem_limit_bytes=limit),
    )(*args)


def shards(params, grad_parts, row_moment, col_moment):
    rows, width = params.shape
    height = width // LANES
    padded = -(-height // 16) * 16
    early = EARLY * BLOCK
    count = len(steps(width))

    held = pltpu.with_memory_space_constraint(grad_parts, HBM)
    (outgoing,) = call(
        half_kernel, [HBM], [(VMEM, shape((rows, width), bf16))], [dma((count,))],
        (held,), 4 * rows * width,
    )
    got = lax.ppermute(outgoing, "dp", SWAP)
    ahead, weight_part = call(
        prepare_kernel, [HBM, HBM, HBM],
        [(HBM, shape((rows, 2 * early), bf16)), (VMEM, shape((1, 1), f32))],
        [VMEM((rows, width), f32), VMEM((rows, early), bf16), VMEM((rows, early), bf16), dma((count + 1,)), dma((2,))],
        (held, params, outgoing), 4 * rows * (width + early),
    )
    ahead = lax.ppermute(ahead, "dp", SWAP)

    gradient, row_part, sent = call(
        sums_kernel, [HBM, VMEM, VMEM, VMEM],
        [(VMEM, shape((rows, width), f32)), (VMEM, shape((1, rows), f32)),
         (VMEM, shape((16, padded, LANES), bf16))],
        [VMEM((rows, width), bf16), VMEM((padded, LANES), f32), dma((count,))],
        (grad_parts, got, row_moment.reshape(1, rows), weight_part), 8 * rows * width,
    )
    col_parts = lax.all_to_all(sent, "row", 0, 0)
    new_cols, cols_copy, old_rows, sent = call(
        moments_kernel, [VMEM] * 4,
        [(VMEM, shape((height, LANES), f32)), (VMEM, shape((height, LANES), f32)),
         (VMEM, shape((16, LANES), f32)), (VMEM, shape((128, 4, LANES), bf16))],
        [VMEM((height, LANES), f32)] * 2, (gradient, col_parts, row_part, col_moment.reshape(2 * height, LANES)),
        4 * rows * width,
    )
    parts = lax.all_to_all(sent, ("dp", "row", "col"), 0, 0)

    n = LATE[0] * BLOCK
    out, new_rows, clip_factor, param_scale, step_size, row_scale, col_scale, early_scale = call(
        first_weights_kernel, [VMEM, VMEM, VMEM, VMEM, HBM],
        [(VMEM, shape((rows, n), bf16)), (VMEM, shape((1, rows), f32)),
         (VMEM, shape((1, 1), f32)), (VMEM, shape((1, 1), f32)), (VMEM, shape((1, 1), f32)),
         (VMEM, shape((rows, LANES), f32)), (VMEM, shape((height, LANES), f32)), (VMEM, shape((32, LANES), f32))],
        [VMEM((rows, n), f32), VMEM((16, LANES), f32), dma],
        (parts, cols_copy, old_rows, gradient, params), 8 * rows * n,
    )
    late = [lax.ppermute(out, "dp", SWAP)]
    start = early + n
    for blocks in LATE[1:]:
        n = blocks * BLOCK
        (out,) = call(
            functools.partial(weights_kernel, start), [VMEM, HBM, VMEM, VMEM, VMEM],
            [(VMEM, shape((rows, n), bf16))], [VMEM((rows, n), f32), dma],
            (gradient, params, row_scale, col_scale, step_size), 8 * rows * n,
        )
        late.append(lax.ppermute(out, "dp", SWAP))
        start += n

    out_shape = shape((rows, 2 * width), bf16)
    new_params, update, new_weights = call(
        params_kernel, [VMEM, HBM, VMEM, VMEM, VMEM],
        [(HBM, shape((rows, width), f32)), (HBM, shape((rows, width), f32)), (HBM, out_shape)],
        [VMEM((rows, width), f32)] * 3 + [VMEM((rows, width), bf16), dma((count,)), dma((3 * count,))],
        (gradient, params, row_scale, col_scale, step_size), 18 * rows * width,
    )
    (new_weights,) = call(
        functools.partial(early_kernel, width), [HBM, HBM, VMEM, VMEM, VMEM, HBM], [(HBM, out_shape)],
        [VMEM((rows, early), bf16), VMEM((rows, 2 * early), bf16), VMEM((rows, early), bf16), dma((2,)), dma],
        (grad_parts, ahead, row_scale, early_scale, step_size, new_weights), 8 * rows * early, {5: 0},
    )
    start = early
    for blocks, values in zip(LATE, late):
        n = blocks * BLOCK
        (new_weights,) = call(
            functools.partial(place_kernel, start, width), [VMEM, HBM], [(HBM, out_shape)],
            [dma], (values, new_weights), 4 * rows * n, {1: 0},
        )
        start += n
    return (
        new_params, new_weights, new_rows.reshape(rows), new_cols.reshape(width), update,
        clip_factor.reshape(()), param_scale.reshape(()),
    )


def solution(mesh):
    in_specs = (P("row", ("col", "dp")), P("dp", "row", "col"), P("row"), P("col"))
    out_specs = (
        P("row", ("col", "dp")),
        P("row", "col"),
        P("row"),
        P(("col", "dp")),
        P("row", ("col", "dp")),
        P(),
        P(),
    )
    return jax.shard_map(shards, mesh=mesh, in_specs=in_specs, out_specs=out_specs, check_vma=False)
```
